32 devices in a mesh: gx: 8 (over z, y), gy: 4 (over x, core).
Axes of the slice: x: 2, y: 2, z: 4, core: 2. Of those that a mesh axis runs over, the one named last changes fastest.
Arguments:
- ocean_temp: float32 [64, 32, 1024], P(None, 'gy', 'gx'), may hold values from -2 to 1.5
- ocean_salt: float32 [64, 32, 1024], P(None, 'gy', 'gx'), may hold values from 33.8 to 34.8
- wet_mask: int32 [64, 32, 1024], P(None, 'gy', 'gx'), may hold values 0 or 1
- vertical_mix: float32 [32, 1024], P('gy', 'gx'), may hold values from 0.05 to 0.3
- friction: float32 [32, 1024], P('gy', 'gx'), may hold values from 0.5 to 5
- pressure: float32 [32, 1024], P('gy', 'gx'), may hold values from 200 to 1500
- pair_column: int32 [16384, 128], P(('gx', 'gy')), may hold values from 0 to 1023
- pair_weight: float32 [16384, 128], P(('gx', 'gy')), may hold values from 0.05 to 1
- block_owner: int32 [16384, 1], P(('gx', 'gy')), may hold values from 0 to 31; in each aligned block of 512 rows (0 to 511, 512 to 1023, ...) at most 32 rows name the same one
- block_target: int32 [16384], P(('gx', 'gy')), may hold values from 0 to 31
- enthalpy: float32 [40, 131072], P(None, ('gx', 'gy')), may hold values from -1 to 0.2
- surface_enthalpy: float32 [131072], P(('gx', 'gy')), may hold values from -1.5 to -0.5
- transition_layer: int32 [131072], P(('gx', 'gy')), may hold values from 0 to 40
- column_area: float32 [131072], P(('gx', 'gy')), may hold values from 0.5 to 2
Outputs:
- new_temp: float32 [64, 32, 1024], P(None, 'gy', 'gx')
- new_salt: float32 [64, 32, 1024], P(None, 'gy', 'gx')
- new_enthalpy: float32 [40, 131072], P(None, ('gx', 'gy'))
- ice_melt: float32 [131072], P(('gx', 'gy'))
The draws below stay inside these ranges and needn't reach their ends.
Inputs may be any that keep to these rules, and one draw needn't show every extreme that they name: `block_owner`: of the 512 blocks of one device at most 32 name the same owner, and some owner gets exactly 32 of them.
All inputs are finite; a program needn't handle non-finite values. No bound on the sum of `wet_mask` on one device may be relied on, other than what follows from the above.
Results may differ from the reference program's by a relative error of at most 0.000059.
Values sent between devices are 32-bit elements; how exact they have to be, the bound alone decides.
A program may use at most 64 MiB of HBM per device.

```python
import math
import jax
import jax.numpy as jnp
import numpy as np
from jax import lax

KL = 64
NL = 40
BW = 128
CJ = 8
CI = 128
NBLK = 512
ICEBLK = 32
CAP = 32
NJ = 32
NI = 1024
IC_DEV = 4096
ICE = 131072
BLOCKS = 16384
N_GY = 4
DEVICES = 32


def touch_ends(values, own_key, smallest, largest):
    shape = values.shape
    place = [jax.random.randint(jax.random.fold_in(own_key, axis), (), 0, shape[axis]) for axis in range(len(shape))]
    values = values.at[tuple(place)].set(smallest)
    longest = shape.index(max(shape))
    place[longest] = (place[longest] + 1) % shape[longest]
    return values.at[tuple(place)].set(largest)


def level_of(own_key, dims, pieces, low, high):
    factor_of, own = 1.0, jax.random.fold_in(own_key, 6)
    for axis_at, shards_of in pieces:
        draws = jnp.exp(jax.random.uniform(jax.random.fold_in(own, axis_at), (shards_of,), jnp.float32, low / len(pieces), high / len(pieces)))
        factor_of = factor_of * jnp.repeat(draws, dims[axis_at] // shards_of).reshape([-1 if axis == axis_at else 1 for axis in range(len(dims))])
    return factor_of


def deal_out(rng, own, number, rows, number_of, top, most, slope):
    order = jax.random.permutation(rng, number_of)
    crowded, common = shares(number_of, rows * top, most, slope, True), shares(number_of, rows * top, most, slope, False)
    places = jnp.arange(number_of)

    def named(lengths, turn):
        used = int((lengths > 0).sum())
        fixed = max(1, used // 4)
        shifted = fixed + (places - fixed + turn * (used - fixed)) % max(1, number_of - fixed)
        return jnp.zeros((number_of,), jnp.int32).at[order[jnp.where(places < fixed, places, shifted)]].set(jnp.asarray(lengths, jnp.int32))

    lengths = jnp.where(number % 4 == 0, named(crowded, number // 4), named(common, number - number // 4 - 1))
    mixed = jax.random.permutation(jax.random.fold_in(own, 3), number_of)
    giver, taker = mixed[0:number_of // 2 * 2:2], mixed[1:number_of // 2 * 2:2]
    margin = jnp.minimum(lengths[giver] - 1, most - lengths[taker]) // 2
    margin = jnp.where((giver == order[0]) | (taker == order[0]) | (lengths[taker] == 0), 0, jnp.maximum(margin, 0))
    shifted = jax.random.randint(jax.random.fold_in(own, 4), (number_of // 2,), 0, 1 << 20) % (margin + 1)
    lengths = lengths.at[giver].add(-shifted).at[taker].add(shifted)
    members = jnp.searchsorted(jnp.cumsum(lengths), jnp.arange(rows * top), side="right").astype(jnp.int32)
    grid = members.reshape(top, rows).T
    grid = grid[jax.random.permutation(jax.random.fold_in(own, 1), rows)]
    turn = jax.random.randint(jax.random.fold_in(own, 2), (rows, 1), 0, top)
    return jnp.take_along_axis(grid, (jnp.arange(top)[None, :] + turn) % top, axis=1)


def shares(count, total, reach, skew, full):
    weights = [(1 << 20) // math.isqrt(rank ** skew) + 1 for rank in range(1, count + 1)]
    largest = reach if full else min(reach, max(-(-total // count), total * weights[0] // sum(weights)))
    least = 1 if total - largest >= count - 1 else 0
    holding, surplus = [largest] + [least] * (count - 1), total - largest - least * (count - 1)
    while surplus > 0:
        candidates = [i for i in range(1, count) if holding[i] < largest] or [i for i in range(1, count) if holding[i] < reach]
        whole, remaining = sum([weights[i] for i in candidates]), surplus
        for i in candidates:
            more = min(reach - holding[i], max(1, remaining * weights[i] // whole), surplus)
            holding[i] = holding[i] + more
            surplus = surplus - more
    return np.array(holding)


def setup_inputs(seed: int = 0) -> dict:
    keys = jax.random.split(jax.random.key(seed), 15)
    ocean_temp = jnp.clip(-2.0 + 3.5 * jax.random.uniform(keys[0], (KL, NJ, NI), jnp.float32) ** level_of(keys[0], (KL, NJ, NI), ((1, 4), (2, 8)), -0.2, 0.2), -2.0, 1.5)
    ocean_salt = jnp.clip(33.8 + 1.0 * jax.random.uniform(keys[1], (KL, NJ, NI), jnp.float32) ** level_of(keys[1], (KL, NJ, NI), ((1, 4), (2, 8)), -0.2, 0.2), 33.8, 34.8)
    wet_mask = touch_ends((jax.random.randint(keys[2], (KL, NJ, NI), 0, 8) < 7).astype(jnp.int32), jax.random.fold_in(keys[2], 1), 0, 1)
    vertical_mix = jnp.clip(0.05 + 0.25 * jax.random.uniform(keys[3], (NJ, NI), jnp.float32) ** level_of(keys[3], (NJ, NI), ((0, 4), (1, 8)), -0.2, 0.2), 0.05, 0.3)
    friction = jnp.clip(jnp.exp(math.log(5.0) - 2.3025851 * jax.random.uniform(keys[4], (NJ, NI), jnp.float32) ** level_of(keys[4], (NJ, NI), ((0, 4), (1, 8)), -0.2, 0.2)), 0.5, 5.0)
    pressure = jnp.clip(200.0 + 1300.0 * jax.random.uniform(keys[5], (NJ, NI), jnp.float32) ** level_of(keys[5], (NJ, NI), ((0, 4), (1, 8)), -0.2, 0.2), 200.0, 1500.0)
    pair_column = touch_ends(jax.random.randint(keys[6], (BLOCKS, BW), 0, CJ * CI), jax.random.fold_in(keys[6], 1), 0, (CJ * CI) - 1).astype(jnp.int32)
    pair_weight = jnp.clip(jnp.exp(math.log(1.0) - 2.9957323 * jax.random.uniform(keys[7], (BLOCKS, BW), jnp.float32) ** level_of(keys[7], (BLOCKS, BW), ((0, 32),), -0.2, 0.2)), 0.05, 1.0)
    block_owner_keys = jax.random.split(jax.random.fold_in(keys[8], 1), BLOCKS // NBLK)
    block_owner_turns = jax.random.permutation(jax.random.fold_in(keys[8], 3), BLOCKS // NBLK)
    block_owner = jax.vmap(lambda own, number: deal_out(jax.random.fold_in(keys[8], 2), own, number, NBLK, DEVICES, 1, CAP, 2))(block_owner_keys, block_owner_turns).reshape((BLOCKS, 1))
    block_target = touch_ends(jax.random.randint(keys[9], (BLOCKS,), 0, ICEBLK), jax.random.fold_in(keys[9], 1), 0, ICEBLK - 1).astype(jnp.int32)
    enthalpy = jnp.clip(-1.0 + 1.2 * jax.random.uniform(keys[10], (NL, ICE), jnp.float32) ** level_of(keys[10], (NL, ICE), ((1, 32),), -0.2, 0.2), -1.0, 0.2)
    surface_enthalpy = jnp.clip(-1.5 + 1.0 * jax.random.uniform(keys[11], (ICE,), jnp.float32) ** level_of(keys[11], (ICE,), ((0, 32),), -0.2, 0.2), -1.5, -0.5)
    transition_layer = touch_ends(jax.random.randint(keys[12], (ICE,), 0, NL + 1), jax.random.fold_in(keys[12], 1), 0, NL).astype(jnp.int32)
    column_area = jnp.clip(jnp.exp(math.log(2.0) - 1.3862944 * jax.random.uniform(keys[13], (ICE,), jnp.float32) ** level_of(keys[13], (ICE,), ((0, 32),), -0.2, 0.2)), 0.5, 2.0)
    return dict(ocean_temp=ocean_temp, ocean_salt=ocean_salt, wet_mask=wet_mask, vertical_mix=vertical_mix, friction=friction, pressure=pressure, pair_column=pair_column, pair_weight=pair_weight, block_owner=block_owner, block_target=block_target, enthalpy=enthalpy, surface_enthalpy=surface_enthalpy, transition_layer=transition_layer, column_area=column_area)


mixing_rate = 0.2
liquidus_slope = -0.0573
liquidus_base = 0.0832
liquidus_depth = -0.000753
latent_ratio = 4.0
salt_ratio = 35.0
relax_rate = 0.1
cold_rate = 2.0
temperate_rate = 0.2

def spread_sideways(extended, wet_ext):
    middle = extended[:, :, 1:-1, 1:-1]
    wet_mid = wet_ext[:, 1:-1, 1:-1]
    height = middle.shape[2]
    breadth = middle.shape[3]
    change = jnp.zeros_like(middle)
    for row_off, col_off in ((0, 1), (2, 1), (1, 0), (1, 2)):
        beside = extended[:, :, row_off:row_off + height, col_off:col_off + breadth]
        wet_beside = wet_ext[:, row_off:row_off + height, col_off:col_off + breadth]
        change = change + (wet_mid * wet_beside)[None] * (beside - middle)
    return middle + mixing_rate * change

def mix_vertical(fields, wetness, vertical_mix):
    link = wetness[:-1] * wetness[1:]
    level_flux = vertical_mix[None, None] * link[None] * (fields[:, 1:] - fields[:, :-1])
    return fields + jnp.pad(level_flux, ((0, 0), (0, 1), (0, 0), (0, 0))) - jnp.pad(level_flux, ((0, 0), (1, 0), (0, 0), (0, 0)))

def shelf_melt(surface_temp, surface_salt, friction, pressure, wet_top):
    heat_gain = jnp.where(wet_top > 0, friction, 1.0)
    salt_safe = jnp.where(wet_top > 0, surface_salt, 34.0)
    salt_gain = heat_gain / salt_ratio
    curvature = heat_gain * liquidus_slope
    linear = heat_gain * (surface_temp - liquidus_base - liquidus_depth * pressure) + latent_ratio * salt_gain
    constant = latent_ratio * salt_gain * salt_safe
    boundary_salt = 2.0 * constant / (linear + jnp.sqrt(linear * linear - 4.0 * curvature * constant))
    boundary_temp = liquidus_slope * boundary_salt + liquidus_base + liquidus_depth * pressure
    heat_flux = heat_gain * (surface_temp - boundary_temp) * wet_top
    salt_flux = salt_gain * (salt_safe - boundary_salt) * wet_top
    return (heat_flux, salt_flux, boundary_temp * wet_top)

def ocean_update(extended, wet_ext, vertical_mix, friction, pressure):
    fields = spread_sideways(extended, wet_ext)
    wetness = wet_ext[:, 1:-1, 1:-1]
    fields = mix_vertical(fields, wetness, vertical_mix)
    heat_flux, salt_flux, base_temp = shelf_melt(fields[0, 0], fields[1, 0], friction, pressure, wetness[0])
    top_level = jnp.stack([fields[0, 0] - relax_rate * heat_flux, fields[1, 0] - relax_rate * salt_flux])
    fields = fields.at[:, 0].set(top_level)
    return (fields, heat_flux / latent_ratio, base_temp)

def solve_columns(enthalpy, transition_layer, surface_enthalpy, cover_sum, base_sum):
    layers = enthalpy.shape[0]
    level = jnp.arange(layers, dtype=jnp.int32)[:, None]
    rate = jnp.where(level < transition_layer[None, :], cold_rate, temperate_rate).astype(jnp.float32)
    inner = 0.5 * (rate[:-1] + rate[1:])
    zero_row = jnp.zeros_like(rate[:1])
    lower = jnp.concatenate([rate[:1], inner], axis=0)
    upper = jnp.concatenate([inner, cover_sum[None, :]], axis=0)
    diagonal = 1.0 + lower + upper
    below = -jnp.concatenate([zero_row, inner], axis=0)
    above = -jnp.concatenate([inner, zero_row], axis=0)
    right_side = enthalpy.at[0].add(rate[0] * surface_enthalpy).at[layers - 1].add(base_sum)

    def forward(carry, items):
        ratio_prev, value_prev = carry
        diag_now, below_now, above_now, side_now = items
        pivot = diag_now - below_now * ratio_prev
        ratio_now = above_now / pivot
        value_now = (side_now - below_now * value_prev) / pivot
        return ((ratio_now, value_now), (ratio_now, value_now))
    start = (jnp.zeros_like(rate[0]), jnp.zeros_like(rate[0]))
    unused, (ratios, values) = lax.scan(forward, start, (diagonal, below, above, right_side))

    def backward(next_value, items):
        ratio_now, value_now = items
        result = value_now - ratio_now * next_value
        return (result, result)
    unused_last, solved = lax.scan(backward, jnp.zeros_like(rate[0]), (ratios, values), reverse=True)
    return solved

def reference(ocean_temp, ocean_salt, wet_mask, vertical_mix, friction, pressure, pair_column, pair_weight, block_owner, block_target, enthalpy, surface_enthalpy, transition_layer, column_area):
    wetness = wet_mask.astype(jnp.float32)
    wet_ext = jnp.pad(wetness, ((0, 0), (1, 1), (1, 1)))
    fields = jnp.stack([ocean_temp, ocean_salt])
    melt_total = jnp.zeros_like(friction)
    base_total = jnp.zeros_like(friction)
    for step in range(2):
        extended = jnp.pad(fields, ((0, 0), (0, 0), (1, 1), (1, 1)))
        fields, melt_rate, base_temp = ocean_update(extended, wet_ext, vertical_mix, friction, pressure)
        melt_total = melt_total + melt_rate
        base_total = base_total + base_temp
    mean_melt = (0.5 * melt_total).reshape(-1)
    mean_base = (0.5 * base_total).reshape(-1)
    device = jnp.arange(BLOCKS, dtype=jnp.int32) // NBLK
    tile_col = device // N_GY
    tile_row = device % N_GY
    cell_row = pair_column // CI
    cell_col = pair_column % CI
    ocean_index = (tile_row[:, None] * CJ + cell_row) * NI + tile_col[:, None] * CI + cell_col
    ice_index = block_owner[:, 0][:, None] * IC_DEV + block_target[:, None] * BW + jnp.arange(BW, dtype=jnp.int32)[None, :]
    flat_ice = ice_index.reshape(-1)
    melt_terms = (pair_weight * mean_melt[ocean_index]).reshape(-1)
    base_terms = (pair_weight * mean_base[ocean_index]).reshape(-1)
    melt_sum = jax.ops.segment_sum(melt_terms, flat_ice, num_segments=ICE) / column_area
    base_sum = jax.ops.segment_sum(base_terms, flat_ice, num_segments=ICE) / column_area
    cover_sum = jax.ops.segment_sum(pair_weight.reshape(-1), flat_ice, num_segments=ICE) / column_area
    new_enthalpy = solve_columns(enthalpy, transition_layer, surface_enthalpy, cover_sum, base_sum)
    return (fields[0], fields[1], new_enthalpy, melt_sum)
```

```python
import functools

import jax
import jax.numpy as jnp
from jax import lax
from jax.experimental import pallas as pl
from jax.experimental.pallas import tpu as pltpu
from jax.sharding import PartitionSpec as P

mixing_rate = 0.2
liquidus_slope = -0.0573
liquidus_base = 0.0832
liquidus_depth = -0.000753
latent_ratio = 4.0
salt_ratio = 35.0
relax_rate = 0.1
cold_rate = 2.0
temperate_rate = 0.2

MESH = pl.DeviceIdType.MESH
CHUNK = 8


def shelf_melt(surface_temp, surface_salt, friction, pressure, wet_top):
    heat_gain = jnp.where(wet_top > 0, friction, 1.0)
    salt_safe = jnp.where(wet_top > 0, surface_salt, 34.0)
    salt_gain = heat_gain / salt_ratio
    curvature = heat_gain * liquidus_slope
    linear = (
        heat_gain * (surface_temp - liquidus_base - liquidus_depth * pressure)
        + latent_ratio * salt_gain
    )
    constant = latent_ratio * salt_gain * salt_safe
    boundary_salt = (
        2.0 * constant / (linear + jnp.sqrt(linear * linear - 4.0 * curvature * constant))
    )
    boundary_temp = liquidus_slope * boundary_salt + liquidus_base + liquidus_depth * pressure
    heat_flux = heat_gain * (surface_temp - boundary_temp) * wet_top
    salt_flux = salt_gain * (salt_safe - boundary_salt) * wet_top
    return (heat_flux, salt_flux, boundary_temp * wet_top)


def digits(axis, size):
    found = []
    base = 1
    while size > 1:
        radix = next(p for p in range(2, size + 1) if size % p == 0)
        found.append((axis, base, radix))
        base *= radix
        size //= radix
    return found


def stage_orders(nx, ny):
    gy = digits("gy", ny)
    gx = digits("gx", nx)
    first = gy + gx
    second = gy[:1] + gx[:1] + gy[1:] + gx[1:]
    return (first, second)


def slot_of(owner, order, ny):
    coord = {"gx": owner // ny, "gy": owner % ny}
    place = jnp.zeros_like(owner)
    for axis, base, radix in order:
        place = place * radix + (coord[axis] // base) % radix
    return place


def live_rows(order, total):
    rows = [total]
    for _, _, radix in order:
        rows.append(rows[-1] // radix)
    return rows


def split_two(value):
    high = value.astype(jnp.bfloat16)
    low = (value - high.astype(jnp.float32)).astype(jnp.bfloat16)
    return high, low


def kernel(sizes, orders, *refs):
    nx, ny, levels, cj, ci, targets, layers = sizes
    refs = list(refs)

    def take(count):
        out = refs[:count]
        del refs[:count]
        return out

    (temp, salt, wet, vmix, fric, pres, pcol, pw, seg_a, seg_b, enth, surf, trans, area) = take(14)
    (out_temp, out_salt, out_enth, out_melt) = take(4)
    (wetp, coef, mid, edge, first) = take(5)
    (row_send, row_recv, col_send, col_recv) = take(4)
    (row_send2, row_recv2, col_send2, col_recv2) = take(4)
    (hot, pay, ratios, values) = take(4)
    chains = []
    for order in (orders[0], orders[1], orders[0]):
        live = take(len(order) + 1)
        got = take(len(order))
        send_sem, recv_sem = take(2)
        chains.append((order, live, got, send_sem, recv_sem))
    (halo_send, halo_recv) = take(2)

    gx = lax.axis_index("gx")
    gy = lax.axis_index("gy")
    coord = {"gx": gx, "gy": gy}
    span = cj * CHUNK
    chunks = levels // CHUNK
    cells = levels * cj
    blocks = pcol.shape[0]
    width = pcol.shape[1]

    sides = (
        (gy > 0, {"gy": gy - 1}),
        (gy < ny - 1, {"gy": gy + 1}),
        (gx > 0, {"gx": gx - 1}),
        (gx < nx - 1, {"gx": gx + 1}),
    )

    for buf in (row_recv, row_recv2):
        for side in range(2):
            @pl.when(jnp.logical_not(sides[side][0]))
            def _():
                buf[side] = jnp.zeros(buf.shape[1:], jnp.float32)
    for buf in (col_recv, col_recv2):
        for side in range(2):
            @pl.when(jnp.logical_not(sides[2 + side][0]))
            def _():
                buf[side] = jnp.zeros(buf.shape[1:], jnp.float32)

    barrier = pltpu.get_barrier_semaphore()
    partners = 0
    for there, device in sides:
        @pl.when(there)
        def _():
            pl.semaphore_signal(barrier, inc=1, device_id=device, device_id_type=MESH)
        partners = partners + there.astype(jnp.int32)
    for axis, base, radix in orders[0]:
        mine = (coord[axis] // base) % radix
        for j in range(1, radix):
            peer = {axis: coord[axis] + ((mine + j) % radix - mine) * base}
            pl.semaphore_signal(barrier, inc=1, device_id=peer, device_id_type=MESH)
            partners = partners + 1

    zeros_pad = jnp.zeros((cj, ci), jnp.float32)
    wetp[pl.ds(0, cj), :] = zeros_pad
    wetp[pl.ds(cj + cells, cj), :] = zeros_pad
    wetp[pl.ds(cj, cells), :] = wet[...].astype(jnp.float32)
    for q in range(2):
        mid[q, pl.ds(0, cj), :] = zeros_pad
        mid[q, pl.ds(cj + cells, cj), :] = zeros_pad

    def pack(q, source, offset, rows, cols):
        rows[0, q] = source[pl.ds(offset, levels, stride=cj), :]
        rows[1, q] = source[pl.ds(offset + cj - 1, levels, stride=cj), :]
        turned = source[pl.ds(offset, cells), :].T
        cols[0, pl.ds(q, 1), :] = turned[0:1]
        cols[1, pl.ds(q, 1), :] = turned[ci - 1 : ci]

    for cols in (col_send, col_send2):
        cols[...] = jnp.zeros(cols.shape, jnp.float32)
    pack(0, temp, 0, row_send, col_send)
    pack(1, salt, 0, row_send, col_send)
    pack(2, wetp, cj, row_send, col_send)

    pl.semaphore_wait(barrier, partners)

    def halo(step, rows, rows_in, cols, cols_in):
        copies = []
        for side, (there, device) in enumerate(sides):
            src, dst = (rows, rows_in) if side < 2 else (cols, cols_in)
            copies.append(
                pltpu.make_async_remote_copy(
                    src_ref=src.at[side % 2],
                    dst_ref=dst.at[1 - side % 2],
                    send_sem=halo_send.at[step, side],
                    recv_sem=halo_recv.at[step, side - side % 2 + 1 - side % 2],
                    device_id=device,
                    device_id_type=MESH,
                )
            )
        return copies

    def halo_start(copies):
        for (there, _), copy in zip(sides, copies):
            @pl.when(there)
            def _():
                copy.start()

    def halo_wait(copies):
        for side, (there, _) in enumerate(sides):
            opposite = copies[side - side % 2 + 1 - side % 2]

            @pl.when(there)
            def _():
                opposite.wait_recv()

    def halo_done(copies):
        for (there, _), copy in zip(sides, copies):
            @pl.when(there)
            def _():
                copy.wait_send()

    halo1 = halo(0, row_send, row_recv, col_send, col_recv)
    halo_start(halo1)

    def make_copies(chain, stage):
        order, live, got, send_sem, recv_sem = chain
        axis, base, radix = order[stage]
        rows = live[stage + 1].shape[0]
        mine = (coord[axis] // base) % radix
        copies = []
        for j in range(1, radix):
            digit = (mine + j) % radix
            copies.append(
                pltpu.make_async_remote_copy(
                    src_ref=live[stage].at[pl.ds(digit * rows, rows)],
                    dst_ref=got[stage].at[j - 1],
                    send_sem=send_sem.at[stage, j - 1],
                    recv_sem=recv_sem.at[stage, j - 1],
                    device_id={axis: coord[axis] + (digit - mine) * base},
                    device_id_type=MESH,
                )
            )
        return copies

    def start_stage(chain, stage):
        for copy in make_copies(chain, stage):
            copy.start()

    def end_stage(chain, stage):
        order, live, got, _, _ = chain
        axis, base, radix = order[stage]
        rows = live[stage + 1].shape[0]
        mine = (coord[axis] // base) % radix
        total = live[stage][pl.ds(pl.multiple_of(mine * rows, rows), rows), :]
        for copy in make_copies(chain, stage):
            copy.wait_recv()
        for j in range(1, radix):
            total = total + got[stage][j - 1]
        live[stage + 1][...] = total
        if stage + 1 < len(order):
            start_stage(chain, stage + 1)

    def drain(chain):
        for stage in range(len(chain[0])):
            for copy in make_copies(chain, stage):
                copy.wait_send()

    seg_total = chains[0][1][0].shape[0]
    hot_rows = 256

    def build_hot(which, seg):
        def body(i, carry):
            start = pl.multiple_of(i * hot_rows, hot_rows)
            row = lax.broadcasted_iota(jnp.int32, (hot_rows, blocks), 0) + start
            hit = (row == seg[...]).astype(jnp.float32)
            hot[which, pl.ds(start, hot_rows), :] = hit.astype(jnp.bfloat16)
            return carry

        lax.fori_loop(0, seg_total // hot_rows, body, 0)

    def sum_blocks(which, slot, target):
        def body(i, carry):
            start = pl.multiple_of(i * hot_rows, hot_rows)
            both = jnp.dot(
                hot[which, pl.ds(start, hot_rows), :],
                pay[slot],
                preferred_element_type=jnp.float32,
            )
            target[pl.ds(start, hot_rows), :] = both[:, :width] + both[:, width:]
            return carry

        lax.fori_loop(0, seg_total // hot_rows, body, 0)

    build_hot(0, seg_a)
    high, low = split_two(pw[...])
    pay[2, :, pl.ds(0, width)] = high
    pay[2, :, pl.ds(width, width)] = low
    sum_blocks(0, 2, chains[2][1][0])
    start_stage(chains[2], 0)
    build_hot(1, seg_b)

    lane = lax.broadcasted_iota(jnp.int32, (CHUNK, cj, ci), 2)
    row = lax.broadcasted_iota(jnp.int32, (CHUNK, cj, ci), 1)

    def spread_edge(q, cols_in):
        turned = lax.broadcasted_iota(jnp.int32, (ci, cells), 0)
        both = jnp.where(turned == 0, cols_in[0, pl.ds(q, 1), :], cols_in[1, pl.ds(q, 1), :])
        edge[q] = both.T

    def around(x, q, c, rows_in):
        start = pl.multiple_of(c * span, span)
        level = pl.ds(pl.multiple_of(c * CHUNK, CHUNK), CHUNK)
        side = edge[q, pl.ds(start, span), :].reshape(CHUNK, cj, ci)
        west = jnp.where(lane == 0, side, pltpu.roll(x, 1, 2))
        east = jnp.where(lane == ci - 1, side, pltpu.roll(x, ci - 1, 2))
        north = jnp.where(row == 0, rows_in[0, q, level, :][:, None, :], pltpu.roll(x, 1, 1))
        south = jnp.where(
            row == cj - 1, rows_in[1, q, level, :][:, None, :], pltpu.roll(x, cj - 1, 1)
        )
        return west, east, north, south

    def couple(c, carry):
        start = pl.multiple_of(c * span, span)
        x = wetp[pl.ds(pl.multiple_of(cj + start, cj), span), :].reshape(CHUNK, cj, ci)
        for n, beside in enumerate(around(x, 2, c, row_recv)):
            coef[n, pl.ds(start, span), :] = (mixing_rate * (x * beside)).reshape(span, ci)
        return carry

    def spread(sources, offset, rows_in, c):
        start = pl.multiple_of(c * span, span)
        weights = [coef[n, pl.ds(start, span), :].reshape(CHUNK, cj, ci) for n in range(4)]
        for q in range(2):
            x = sources[q][pl.ds(start, span), :].reshape(CHUNK, cj, ci)
            total = x
            for weight, beside in zip(weights, around(x, q, c, rows_in)):
                total = total + weight * (beside - x)
            mid[q, pl.ds(pl.multiple_of(cj + start, cj), span), :] = total.reshape(span, ci)

    def mix(c, targets_of):
        start = pl.multiple_of(c * span, span)
        up = pl.ds(start, span)
        here = pl.ds(pl.multiple_of(start + cj, cj), span)
        down = pl.ds(pl.multiple_of(start + 2 * cj, cj), span)
        rate = jnp.broadcast_to(vmix[...][None], (CHUNK, cj, ci)).reshape(span, ci)
        wet_here = rate * wetp[here, :]
        link_up = wet_here * wetp[up, :]
        link_down = wet_here * wetp[down, :]
        for q in range(2):
            x = mid[q, here, :]
            targets_of[q][pl.ds(start, span), :] = (
                x + link_down * (mid[q, down, :] - x) - link_up * (x - mid[q, up, :])
            )

    wet_top = wetp[pl.ds(cj, cj), :]

    def surface():
        link = vmix[...] * wet_top * wetp[pl.ds(2 * cj, cj), :]
        top = []
        for q in range(2):
            x = mid[q, pl.ds(cj, cj), :]
            top.append(x + link * (mid[q, pl.ds(2 * cj, cj), :] - x))
        heat, saltf, base_temp = shelf_melt(top[0], top[1], fric[...], pres[...], wet_top)
        return (
            top[0] - relax_rate * heat,
            top[1] - relax_rate * saltf,
            heat / latent_ratio,
            base_temp,
        )

    def loop(low_c, high_c, body):
        def wrapped(c, carry):
            body(c)
            return carry

        lax.fori_loop(low_c, high_c, wrapped, 0)

    halo_wait(halo1)
    for q in range(3):
        spread_edge(q, col_recv)
    lax.fori_loop(0, chunks, couple, 0)
    loop(0, chunks, functools.partial(spread, (temp, salt), 0, row_recv))
    end_stage(chains[2], 0)
    loop(0, chunks, lambda c: mix(c, (first.at[0], first.at[1])))
    top_temp, top_salt, melt_one, base_one = surface()
    first[0, pl.ds(0, cj), :] = top_temp
    first[1, pl.ds(0, cj), :] = top_salt
    for q in range(2):
        pack(q, first.at[q], 0, row_send2, col_send2)
    halo2 = halo(1, row_send2, row_recv2, col_send2, col_recv2)
    halo_start(halo2)

    groups = enth.shape[1] // width
    for g in range(groups):
        values[pl.ds(g * layers, layers), :] = enth[:, g * width : (g + 1) * width]

    def rate_of(k):
        return jnp.where(k < trans[...], cold_rate, temperate_rate).astype(jnp.float32)

    def layer(k):
        return pl.ds(k, groups, stride=layers)

    def eliminate(k, carry):
        ratio, value, rate, inner_up = carry
        rate_next = rate_of(k + 1)
        inner = 0.5 * (rate + rate_next)
        pivot = 1.0 / (1.0 + inner_up + inner + inner_up * ratio)
        value = (values[layer(k), :] + inner_up * value) * pivot
        ratio = -inner * pivot
        values[layer(k), :] = value
        ratios[pl.ds(pl.multiple_of(k * groups, groups), groups), :] = ratio
        return ratio, value, rate_next, inner

    end_stage(chains[2], 1)
    rate_top = rate_of(0)
    rate_next = rate_of(1)
    inner = 0.5 * (rate_top + rate_next)
    pivot = 1.0 / (1.0 + rate_top + inner)
    value = (values[layer(0), :] + rate_top * surf[...]) * pivot
    ratio = -inner * pivot
    values[layer(0), :] = value
    ratios[pl.ds(0, groups), :] = ratio
    half = layers // 2
    state = lax.fori_loop(1, half, eliminate, (ratio, value, rate_next, inner))

    end_stage(chains[2], 2)
    halo_wait(halo2)
    for q in range(2):
        spread_edge(q, col_recv2)
    second = functools.partial(spread, (first.at[0], first.at[1]), 0, row_recv2)
    second(0)
    top_temp, top_salt, melt_two, base_two = surface()
    mean_melt = 0.5 * (melt_one + melt_two)
    mean_base = 0.5 * (base_one + base_two)

    part = 64

    def pairs(i, carry):
        at = pl.ds(pl.multiple_of(i * part, part), part)
        place = pcol[at, :]
        place_row = place // ci
        place_col = place - place_row * ci
        weight = pw[at, :]
        for slot, table in ((0, mean_melt), (1, mean_base)):
            found = jnp.zeros((part, width), jnp.float32)
            for r in range(cj):
                line = jnp.broadcast_to(table[r : r + 1], (part, ci))
                there = jnp.take_along_axis(
                    line, place_col, axis=1, mode="promise_in_bounds"
                )
                found = jnp.where(place_row == r, there, found)
            high, low = split_two(weight * found)
            pay[slot, at, pl.ds(0, width)] = high
            pay[slot, at, pl.ds(width, width)] = low
        return carry

    lax.fori_loop(0, blocks // part, pairs, 0)
    for slot in range(2):
        sum_blocks(slot, slot, chains[slot][1][0])
        start_stage(chains[slot], 0)

    state_box = [state]

    def rest_spread():
        loop(1, chunks, second)

    def rest_mix():
        loop(0, chunks, lambda c: mix(c, (out_temp, out_salt)))
        out_temp[pl.ds(0, cj), :] = top_temp
        out_salt[pl.ds(0, cj), :] = top_salt

    def rest_eliminate():
        state_box[0] = lax.fori_loop(half, layers - 1, eliminate, state_box[0])

    fill = [rest_spread, rest_mix, rest_eliminate]
    stages = len(orders[0])
    cover_stage = 3
    for stage in range(stages):
        if stage < len(fill):
            fill[stage]()
        end_stage(chains[0], stage)
        end_stage(chains[1], stage)
        if cover_stage < stages:
            end_stage(chains[2], cover_stage)
            cover_stage += 1
    for work in fill[stages:]:
        work()

    share = 1.0 / area[...]
    melt_sum = chains[0][1][-1][...] * share
    base_sum = chains[1][1][-1][...] * share
    cover_sum = chains[2][1][-1][...] * share
    out_melt[...] = melt_sum
    ratio, value, rate, inner_up = state_box[0]
    last = layers - 1
    pivot = 1.0 / (1.0 + inner_up + cover_sum + inner_up * ratio)
    solved = (values[layer(last), :] + base_sum + inner_up * value) * pivot
    values[layer(last), :] = solved

    def substitute(n, below):
        k = last - 1 - n
        solved = values[layer(k), :] - ratios[
            pl.ds(pl.multiple_of(k * groups, groups), groups), :
        ] * below
        values[layer(k), :] = solved
        return solved

    lax.fori_loop(0, last, substitute, solved)
    for g in range(groups):
        out_enth[:, g * width : (g + 1) * width] = values[pl.ds(g * layers, layers), :]

    halo_done(halo1)
    halo_done(halo2)
    for chain in chains:
        drain(chain)


def local(
    nx,
    ny,
    ocean_temp,
    ocean_salt,
    wet_mask,
    vertical_mix,
    friction,
    pressure,
    pair_column,
    pair_weight,
    block_owner,
    block_target,
    enthalpy,
    surface_enthalpy,
    transition_layer,
    column_area,
):
    levels, cj, ci = wet_mask.shape
    cells = levels * cj
    blocks, width = pair_column.shape
    layers, columns = enthalpy.shape
    targets = columns // width
    orders = stage_orders(nx, ny)
    owner = block_owner[:, 0]
    segs = [
        (slot_of(owner, order, ny) * targets + block_target).reshape(1, blocks)
        for order in orders
    ]
    f32 = jnp.float32
    total = nx * ny * targets
    scratch = [
        pltpu.VMEM((cells + 2 * cj, ci), f32),
        pltpu.VMEM((4, cells, ci), f32),
        pltpu.VMEM((2, cells + 2 * cj, ci), f32),
        pltpu.VMEM((3, cells, ci), f32),
        pltpu.VMEM((2, cells, ci), f32),
        pltpu.VMEM((2, 3, levels, ci), f32),
        pltpu.VMEM((2, 3, levels, ci), f32),
        pltpu.VMEM((2, 8, cells), f32),
        pltpu.VMEM((2, 8, cells), f32),
        pltpu.VMEM((2, 2, levels, ci), f32),
        pltpu.VMEM((2, 2, levels, ci), f32),
        pltpu.VMEM((2, 8, cells), f32),
        pltpu.VMEM((2, 8, cells), f32),
        pltpu.VMEM((2, total, blocks), jnp.bfloat16),
        pltpu.VMEM((3, blocks, 2 * width), jnp.bfloat16),
        pltpu.VMEM((layers * targets, width), f32),
        pltpu.VMEM((layers * targets, width), f32),
    ]
    for order in (orders[0], orders[1], orders[0]):
        rows = live_rows(order, total)
        scratch += [pltpu.VMEM((n, width), f32) for n in rows]
        scratch += [
            pltpu.VMEM((radix - 1, n, width), f32)
            for (_, _, radix), n in zip(order, rows[1:])
        ]
        most = max(radix for _, _, radix in order) - 1
        scratch += [pltpu.SemaphoreType.DMA((len(order), most))] * 2
    scratch += [pltpu.SemaphoreType.DMA((2, 4))] * 2
    vmem = pl.BlockSpec(memory_space=pltpu.VMEM)
    sizes = (nx, ny, levels, cj, ci, targets, layers)
    new_temp, new_salt, new_enthalpy, ice_melt = pl.pallas_call(
        functools.partial(kernel, sizes, orders),
        out_shape=(
            jax.ShapeDtypeStruct((cells, ci), f32),
            jax.ShapeDtypeStruct((cells, ci), f32),
            jax.ShapeDtypeStruct((layers, columns), f32),
            jax.ShapeDtypeStruct((targets, width), f32),
        ),
        in_specs=[vmem] * 14,
        out_specs=(vmem,) * 4,
        scratch_shapes=scratch,
        compiler_params=pltpu.CompilerParams(
            collective_id=0, has_side_effects=True, vmem_limit_bytes=48 * 1024 * 1024
        ),
    )(
        ocean_temp.reshape(cells, ci),
        ocean_salt.reshape(cells, ci),
        wet_mask.reshape(cells, ci),
        vertical_mix,
        friction,
        pressure,
        pair_column,
        pair_weight,
        segs[0],
        segs[1],
        enthalpy,
        surface_enthalpy.reshape(targets, width),
        transition_layer.reshape(targets, width),
        column_area.reshape(targets, width),
    )
    return (
        new_temp.reshape(levels, cj, ci),
        new_salt.reshape(levels, cj, ci),
        new_enthalpy,
        ice_melt.reshape(columns),
    )


def solution(mesh):
    return jax.shard_map(
        functools.partial(local, mesh.shape["gx"], mesh.shape["gy"]),
        mesh=mesh,
        in_specs=(
            P(None, "gy", "gx"),
            P(None, "gy", "gx"),
            P(None, "gy", "gx"),
            P("gy", "gx"),
            P("gy", "gx"),
            P("gy", "gx"),
            P(("gx", "gy"), None),
            P(("gx", "gy"), None),
            P(("gx", "gy"), None),
            P(("gx", "gy")),
            P(None, ("gx", "gy")),
            P(("gx", "gy")),
            P(("gx", "gy")),
            P(("gx", "gy")),
        ),
        out_specs=(
            P(None, "gy", "gx"),
            P(None, "gy", "gx"),
            P(None, ("gx", "gy")),
            P(("gx", "gy")),
        ),
        check_vma=False,
    )
```

```python
import functools

import jax
import jax.numpy as jnp
from jax import lax
from jax.experimental import pallas as pl
from jax.experimental.pallas import tpu as pltpu
from jax.sharding import PartitionSpec as P

mixing_rate = 0.2
liquidus_slope = -0.0573
liquidus_base = 0.0832
liquidus_depth = -0.000753
latent_ratio = 4.0
salt_ratio = 35.0
relax_rate = 0.1
cold_rate = 2.0
temperate_rate = 0.2

MESH = pl.DeviceIdType.MESH
CHUNK = 8
LIMIT = 62 * 1024 * 1024


def shelf_melt(surface_temp, surface_salt, friction, pressure, wet_top):
    heat_gain = jnp.where(wet_top > 0, friction, 1.0)
    salt_safe = jnp.where(wet_top > 0, surface_salt, 34.0)
    salt_gain = heat_gain / salt_ratio
    curvature = heat_gain * liquidus_slope
    linear = (
        heat_gain * (surface_temp - liquidus_base - liquidus_depth * pressure)
        + latent_ratio * salt_gain
    )
    constant = latent_ratio * salt_gain * salt_safe
    boundary_salt = (
        2.0 * constant / (linear + jnp.sqrt(linear * linear - 4.0 * curvature * constant))
    )
    boundary_temp = liquidus_slope * boundary_salt + liquidus_base + liquidus_depth * pressure
    heat_flux = heat_gain * (surface_temp - boundary_temp) * wet_top
    salt_flux = salt_gain * (salt_safe - boundary_salt) * wet_top
    return (heat_flux, salt_flux, boundary_temp * wet_top)


def digits(axis, size):
    found = []
    base = 1
    while size > 1:
        radix = next(p for p in range(2, size + 1) if size % p == 0)
        if axis == "gx" and size == 4:
            radix = size
        found.append((axis, base, radix))
        base *= radix
        size //= radix
    return found


def stage_orders(nx, ny):
    gy = digits("gy", ny)
    gx = digits("gx", nx)
    first = gy + gx
    second = gy[:1] + gx[:1] + gy[1:] + gx[1:]
    return (first, second)


def slot_of(owner, order, ny):
    coord = {"gx": owner // ny, "gy": owner % ny}
    place = jnp.zeros_like(owner)
    for axis, base, radix in order:
        place = place * radix + (coord[axis] // base) % radix
    return place


def live_rows(order, total):
    rows = [total]
    for _, _, radix in order:
        rows.append(rows[-1] // radix)
    return rows


def split_two(value):
    high = value.astype(jnp.bfloat16)
    low = (value - high.astype(jnp.float32)).astype(jnp.bfloat16)
    return high, low


def kernel(sizes, orders, *refs):
    nx, ny, levels, cj, ci, targets, layers = sizes
    refs = list(refs)

    def take(count):
        out = refs[:count]
        del refs[:count]
        return out

    given = take(14)
    results = take(4)
    held = take(14)
    (out_temp, out_salt, out_enth, out_melt) = made = take(4)
    (load_sem, save_sem) = take(2)
    saves = [
        pltpu.make_async_copy(src, dst, save_sem.at[i])
        for i, (src, dst) in enumerate(zip(made, results))
    ]
    loads = [
        pltpu.make_async_copy(src, dst, load_sem.at[i])
        for i, (src, dst) in enumerate(zip(given, held))
    ]
    for load in loads:
        load.start()
    (temp, salt, wet, vmix, fric, pres, owner, target, pw, trans, surf, enth, pcol, area) = held
    (wetp, coef, mid, edge, first) = take(5)
    (edge_top, first_top, last_layer) = take(3)
    (row_send, row_recv, col_send, col_recv) = take(4)
    (row_send2, row_recv2, col_send2, col_recv2) = take(4)
    (row_top, row_top_in, col_top, col_top_in) = take(4)
    (row_top2, row_top_in2, col_top2, col_top_in2) = take(4)
    (hot, pay, ratios, values) = take(4)
    chains = []
    for order in (orders[0], orders[1], orders[0]):
        live = take(len(order) + 1)
        got = take(len(order))
        send_sem, recv_sem = take(2)
        chains.append((order, live, got, send_sem, recv_sem))
    (halo_send, halo_recv) = take(2)

    gx = lax.axis_index("gx")
    gy = lax.axis_index("gy")
    coord = {"gx": gx, "gy": gy}
    span = cj * CHUNK
    chunks = levels // CHUNK
    cells = levels * cj
    blocks = pcol.shape[0]
    width = pcol.shape[1]

    sides = (
        (gy > 0, {"gy": gy - 1}),
        (gy < ny - 1, {"gy": gy + 1}),
        (gx > 0, {"gx": gx - 1}),
        (gx < nx - 1, {"gx": gx + 1}),
    )

    for buf in (row_recv, row_recv2, row_top_in, row_top_in2):
        for side in range(2):
            @pl.when(jnp.logical_not(sides[side][0]))
            def _():
                buf[side] = jnp.zeros(buf.shape[1:], jnp.float32)
    for buf in (col_recv, col_recv2, col_top_in, col_top_in2):
        for side in range(2):
            @pl.when(jnp.logical_not(sides[2 + side][0]))
            def _():
                buf[side] = jnp.zeros(buf.shape[1:], jnp.float32)

    barrier = pltpu.get_barrier_semaphore()
    partners = 0
    for there, device in sides:
        @pl.when(there)
        def _():
            pl.semaphore_signal(barrier, inc=1, device_id=device, device_id_type=MESH)
        partners = partners + there.astype(jnp.int32)
    for axis, base, radix in orders[0]:
        mine = (coord[axis] // base) % radix
        for j in range(1, radix):
            peer = {axis: coord[axis] + ((mine + j) % radix - mine) * base}
            pl.semaphore_signal(barrier, inc=1, device_id=peer, device_id_type=MESH)
            partners = partners + 1

    zeros_pad = jnp.zeros((cj, ci), jnp.float32)
    wetp[pl.ds(0, cj), :] = zeros_pad
    wetp[pl.ds(cj + cells, cj), :] = zeros_pad
    for q in range(2):
        mid[q, pl.ds(0, cj), :] = zeros_pad
        mid[q, pl.ds(cj + cells, cj), :] = zeros_pad

    def pack(q, source, offset, rows, cols):
        count = rows.shape[2]
        rows[0, q] = source[pl.ds(offset, count, stride=cj), :]
        rows[1, q] = source[pl.ds(offset + cj - 1, count, stride=cj), :]
        turned = source[pl.ds(offset, cols.shape[2]), :].T
        cols[0, pl.ds(q, 1), :] = turned[0:1]
        cols[1, pl.ds(q, 1), :] = turned[ci - 1 : ci]

    for cols in (col_send, col_send2, col_top, col_top2):
        cols[...] = jnp.zeros(cols.shape, jnp.float32)
    first_top[...] = jnp.zeros(first_top.shape, jnp.float32)
    for load in loads[:3]:
        load.wait()
    wetp[pl.ds(cj, cells), :] = wet[...].astype(jnp.float32)

    def pack_all(rows, cols):
        pack(0, temp, 0, rows, cols)
        pack(1, salt, 0, rows, cols)
        pack(2, wetp, cj, rows, cols)

    pack_all(row_top, col_top)
    pl.semaphore_wait(barrier, partners)

    def halo(step, rows, rows_in, cols, cols_in):
        copies = []
        for side, (there, device) in enumerate(sides):
            src, dst = (rows, rows_in) if side < 2 else (cols, cols_in)
            copies.append(
                pltpu.make_async_remote_copy(
                    src_ref=src.at[side % 2],
                    dst_ref=dst.at[1 - side % 2],
                    send_sem=halo_send.at[step, side],
                    recv_sem=halo_recv.at[step, side - side % 2 + 1 - side % 2],
                    device_id=device,
                    device_id_type=MESH,
                )
            )
        return copies

    def halo_start(copies):
        for (there, _), copy in zip(sides, copies):
            @pl.when(there)
            def _():
                copy.start()

    def halo_wait(copies):
        for side, (there, _) in enumerate(sides):
            opposite = copies[side - side % 2 + 1 - side % 2]

            @pl.when(there)
            def _():
                opposite.wait_recv()

    def halo_done(copies):
        for (there, _), copy in zip(sides, copies):
            @pl.when(there)
            def _():
                copy.wait_send()

    halo_top1 = halo(2, row_top, row_top_in, col_top, col_top_in)
    halo_start(halo_top1)
    pack_all(row_send, col_send)
    halo1 = halo(0, row_send, row_recv, col_send, col_recv)
    halo_start(halo1)

    def make_copies(chain, stage):
        order, live, got, send_sem, recv_sem = chain
        axis, base, radix = order[stage]
        rows = live[stage + 1].shape[0]
        mine = (coord[axis] // base) % radix
        copies = []
        for j in range(1, radix):
            digit = (mine + j) % radix
            copies.append(
                pltpu.make_async_remote_copy(
                    src_ref=live[stage].at[pl.ds(digit * rows, rows)],
                    dst_ref=got[stage].at[j - 1],
                    send_sem=send_sem.at[stage, j - 1],
                    recv_sem=recv_sem.at[stage, j - 1],
                    device_id={axis: coord[axis] + (digit - mine) * base},
                    device_id_type=MESH,
                )
            )
        return copies

    def start_stage(chain, stage):
        for copy in make_copies(chain, stage):
            copy.start()

    def end_stage(chain, stage):
        order, live, got, _, _ = chain
        axis, base, radix = order[stage]
        rows = live[stage + 1].shape[0]
        mine = (coord[axis] // base) % radix
        total = live[stage][pl.ds(pl.multiple_of(mine * rows, rows), rows), :]
        for copy in make_copies(chain, stage):
            copy.wait_recv()
        for j in range(1, radix):
            total = total + got[stage][j - 1]
        live[stage + 1][...] = total
        if stage + 1 < len(order):
            start_stage(chain, stage + 1)

    def drain(chain):
        for stage in range(len(chain[0])):
            for copy in make_copies(chain, stage):
                copy.wait_send()

    seg_total = chains[0][1][0].shape[0]
    hot_rows = min(256, seg_total)

    def build_hot(which):
        seg = slot_of(owner[...], orders[which], ny) * targets + target[...]

        def body(i, carry):
            start = pl.multiple_of(i * hot_rows, hot_rows)
            row = lax.broadcasted_iota(jnp.int32, (hot_rows, blocks), 0) + start
            hit = (row == seg).astype(jnp.float32)
            hot[which, pl.ds(start, hot_rows), :] = hit.astype(jnp.bfloat16)
            return carry

        lax.fori_loop(0, seg_total // hot_rows, body, 0)

    def sum_blocks(which, slot, target):
        def body(i, carry):
            start = pl.multiple_of(i * hot_rows, hot_rows)
            both = jnp.dot(
                hot[which, pl.ds(start, hot_rows), :],
                pay[slot],
                preferred_element_type=jnp.float32,
            )
            target[pl.ds(start, hot_rows), :] = both[:, :width] + both[:, width:]
            return carry

        lax.fori_loop(0, seg_total // hot_rows, body, 0)

    for load in loads[6:9]:
        load.wait()
    build_hot(0)
    high, low = split_two(pw[...])
    pay[2, :, pl.ds(0, width)] = high
    pay[2, :, pl.ds(width, width)] = low
    sum_blocks(0, 2, chains[2][1][0])
    start_stage(chains[2], 0)
    for load in loads[3:6]:
        load.wait()

    lane = lax.broadcasted_iota(jnp.int32, (CHUNK, cj, ci), 2)
    row = lax.broadcasted_iota(jnp.int32, (CHUNK, cj, ci), 1)

    def spread_edge(q, cols_in, edge):
        turned = lax.broadcasted_iota(jnp.int32, (ci, cols_in.shape[2]), 0)
        both = jnp.where(turned == 0, cols_in[0, pl.ds(q, 1), :], cols_in[1, pl.ds(q, 1), :])
        edge[q] = both.T

    def around(x, q, c, rows_in, edge):
        start = pl.multiple_of(c * span, span)
        level = pl.ds(pl.multiple_of(c * CHUNK, CHUNK), CHUNK)
        side = edge[q, pl.ds(start, span), :].reshape(CHUNK, cj, ci)
        west = jnp.where(lane == 0, side, pltpu.roll(x, 1, 2))
        east = jnp.where(lane == ci - 1, side, pltpu.roll(x, ci - 1, 2))
        north = jnp.where(row == 0, rows_in[0, q, level, :][:, None, :], pltpu.roll(x, 1, 1))
        south = jnp.where(
            row == cj - 1, rows_in[1, q, level, :][:, None, :], pltpu.roll(x, cj - 1, 1)
        )
        return west, east, north, south

    def couple(rows_in, edge, c):
        start = pl.multiple_of(c * span, span)
        x = wetp[pl.ds(pl.multiple_of(cj + start, cj), span), :].reshape(CHUNK, cj, ci)
        for n, beside in enumerate(around(x, 2, c, rows_in, edge)):
            coef[n, pl.ds(start, span), :] = (mixing_rate * (x * beside)).reshape(span, ci)

    def spread(sources, rows_in, edge, c):
        start = pl.multiple_of(c * span, span)
        weights = [coef[n, pl.ds(start, span), :].reshape(CHUNK, cj, ci) for n in range(4)]
        for q in range(2):
            x = sources[q][pl.ds(start, span), :].reshape(CHUNK, cj, ci)
            total = x
            for weight, beside in zip(weights, around(x, q, c, rows_in, edge)):
                total = total + weight * (beside - x)
            mid[q, pl.ds(pl.multiple_of(cj + start, cj), span), :] = total.reshape(span, ci)

    def mix(c, targets_of):
        start = pl.multiple_of(c * span, span)
        up = pl.ds(start, span)
        here = pl.ds(pl.multiple_of(start + cj, cj), span)
        down = pl.ds(pl.multiple_of(start + 2 * cj, cj), span)
        rate = jnp.broadcast_to(vmix[...][None], (CHUNK, cj, ci)).reshape(span, ci)
        wet_here = rate * wetp[here, :]
        link_up = wet_here * wetp[up, :]
        link_down = wet_here * wetp[down, :]
        for q in range(2):
            x = mid[q, here, :]
            targets_of[q][pl.ds(start, span), :] = (
                x + link_down * (mid[q, down, :] - x) - link_up * (x - mid[q, up, :])
            )

    wet_top = wetp[pl.ds(cj, cj), :]

    def surface():
        link = vmix[...] * wet_top * wetp[pl.ds(2 * cj, cj), :]
        top = []
        for q in range(2):
            x = mid[q, pl.ds(cj, cj), :]
            top.append(x + link * (mid[q, pl.ds(2 * cj, cj), :] - x))
        heat, saltf, base_temp = shelf_melt(top[0], top[1], fric[...], pres[...], wet_top)
        return (
            top[0] - relax_rate * heat,
            top[1] - relax_rate * saltf,
            heat / latent_ratio,
            base_temp,
        )

    def loop(low_c, high_c, body):
        def wrapped(c, carry):
            body(c)
            return carry

        lax.fori_loop(low_c, high_c, wrapped, 0)

    halo_wait(halo_top1)
    for q in range(3):
        spread_edge(q, col_top_in, edge_top)
    couple(row_top_in, edge_top, 0)
    spread((temp, salt), row_top_in, edge_top, 0)
    mix(0, (first_top.at[0], first_top.at[1]))
    top_temp, top_salt, melt_one, base_one = surface()
    first_top[0, pl.ds(0, cj), :] = top_temp
    first_top[1, pl.ds(0, cj), :] = top_salt
    for q in range(2):
        pack(q, first_top.at[q], 0, row_top2, col_top2)
    halo_top2 = halo(3, row_top2, row_top_in2, col_top2, col_top_in2)
    halo_start(halo_top2)

    build_hot(1)
    end_stage(chains[2], 0)
    for load in loads[9:12]:
        load.wait()
    groups = enth.shape[1] // width
    for g in range(groups):
        values[pl.ds(g * layers, layers), :] = enth[:, g * width : (g + 1) * width]

    def rate_of(k):
        return jnp.where(k < trans[...], cold_rate, temperate_rate).astype(jnp.float32)

    def layer(k):
        return pl.ds(k, groups, stride=layers)

    def eliminate(k, carry):
        ratio, value, rate, inner_up = carry
        rate_next = rate_of(k + 1)
        inner = 0.5 * (rate + rate_next)
        pivot = 1.0 / (1.0 + inner_up + inner + inner_up * ratio)
        value = (values[layer(k), :] + inner_up * value) * pivot
        ratio = -inner * pivot
        values[layer(k), :] = value
        ratios[layer(k), :] = ratio
        return ratio, value, rate_next, inner

    rate_top = rate_of(0)
    rate_next = rate_of(1)
    inner = 0.5 * (rate_top + rate_next)
    pivot = 1.0 / (1.0 + rate_top + inner)
    value = (values[layer(0), :] + rate_top * surf[...]) * pivot
    ratio = -inner * pivot
    values[layer(0), :] = value
    ratios[layer(0), :] = ratio
    last = layers - 1
    state = lax.fori_loop(1, last, eliminate, (ratio, value, rate_next, inner))

    halo_wait(halo_top2)
    for q in range(2):
        spread_edge(q, col_top_in2, edge_top)
    spread((first_top.at[0], first_top.at[1]), row_top_in2, edge_top, 0)
    new_top_temp, new_top_salt, melt_two, base_two = surface()
    mean_melt = 0.5 * (melt_one + melt_two)
    mean_base = 0.5 * (base_one + base_two)
    for load in loads[12:]:
        load.wait()

    part = 64

    def pairs(i, carry):
        at = pl.ds(pl.multiple_of(i * part, part), part)
        place = pcol[at, :]
        place_row = place // ci
        place_col = place - place_row * ci
        weight = pw[at, :]
        for slot, table in ((0, mean_melt), (1, mean_base)):
            found = jnp.zeros((part, width), jnp.float32)
            for r in range(cj):
                line = jnp.broadcast_to(table[r : r + 1], (part, ci))
                there = jnp.take_along_axis(
                    line, place_col, axis=1, mode="promise_in_bounds"
                )
                found = jnp.where(place_row == r, there, found)
            high, low = split_two(weight * found)
            pay[slot, at, pl.ds(0, width)] = high
            pay[slot, at, pl.ds(width, width)] = low
        return carry

    lax.fori_loop(0, blocks // part, pairs, 0)
    for slot in range(2):
        sum_blocks(slot, slot, chains[slot][1][0])
        start_stage(chains[slot], 0)

    halo2 = halo(1, row_send2, row_recv2, col_send2, col_recv2)

    def first_spread():
        halo_wait(halo1)
        for q in range(3):
            spread_edge(q, col_recv, edge)
        loop(0, chunks, functools.partial(couple, row_recv, edge))
        loop(0, chunks, functools.partial(spread, (temp, salt), row_recv, edge))

    def first_mix():
        loop(0, chunks, lambda c: mix(c, (first.at[0], first.at[1])))
        first[0, pl.ds(0, cj), :] = top_temp
        first[1, pl.ds(0, cj), :] = top_salt
        for q in range(2):
            pack(q, first.at[q], 0, row_send2, col_send2)
        halo_start(halo2)

    def second_step():
        halo_wait(halo2)
        for q in range(2):
            spread_edge(q, col_recv2, edge)
        sources = (first.at[0], first.at[1])
        loop(0, chunks, functools.partial(spread, sources, row_recv2, edge))
        loop(0, chunks, lambda c: mix(c, (out_temp, out_salt)))
        out_temp[pl.ds(0, cj), :] = new_top_temp
        out_salt[pl.ds(0, cj), :] = new_top_salt
        saves[0].start()
        saves[1].start()

    ratio_end, value_end, rate_end, inner_end = state

    def back_terms():
        ratios[layer(last - 1), :] = -ratio_end

        def body(n, carry):
            level, slope = carry
            k = last - 2 - n
            ratio = ratios[layer(k), :]
            level = values[layer(k), :] - ratio * level
            slope = -ratio * slope
            values[layer(k), :] = level
            ratios[layer(k), :] = slope
            return level, slope

        lax.fori_loop(0, last - 1, body, (value_end, -ratio_end))
        last_side = values[layer(last), :]
        values[layer(last), :] = jnp.zeros((groups, width), jnp.float32)
        ratios[layer(last), :] = jnp.ones((groups, width), jnp.float32)
        return last_side

    side_box = []
    fill = [
        first_spread,
        first_mix,
        lambda: side_box.append(back_terms()),
        second_step,
    ]
    stages = len(orders[0])
    for stage in range(stages):
        if stage < len(fill):
            fill[stage]()
        end_stage(chains[0], stage)
        end_stage(chains[1], stage)
        if stage + 1 < stages:
            end_stage(chains[2], stage + 1)
    for work in fill[stages:]:
        work()

    share = 1.0 / area[...]
    melt_sum = chains[0][1][-1][...] * share
    base_sum = chains[1][1][-1][...] * share
    cover_sum = chains[2][1][-1][...] * share
    out_melt[...] = melt_sum
    pivot = 1.0 / (1.0 + inner_end + cover_sum + inner_end * ratio_end)
    last_layer[...] = (side_box[0] + base_sum + inner_end * value_end) * pivot
    for g in range(groups):
        rows = pl.ds(g * layers, layers)
        solved = values[rows, :] + ratios[rows, :] * last_layer[pl.ds(g, 1), :]
        out_enth[:, g * width : (g + 1) * width] = solved
    saves[2].start()
    saves[3].start()

    halo_done(halo_top1)
    halo_done(halo_top2)
    halo_done(halo1)
    halo_done(halo2)
    for chain in chains:
        drain(chain)
    for save in saves:
        save.wait()


def store(*refs):
    count = len(refs) // 2
    sem = refs[-1]
    copies = [
        pltpu.make_async_copy(src, dst, sem.at[i])
        for i, (src, dst) in enumerate(zip(refs[:count], refs[count:-1]))
    ]
    for copy in copies:
        copy.start()
    for copy in copies:
        copy.wait()


def local(
    nx,
    ny,
    ocean_temp,
    ocean_salt,
    wet_mask,
    vertical_mix,
    friction,
    pressure,
    pair_column,
    pair_weight,
    block_owner,
    block_target,
    enthalpy,
    surface_enthalpy,
    transition_layer,
    column_area,
):
    levels, cj, ci = wet_mask.shape
    cells = levels * cj
    blocks, width = pair_column.shape
    layers, columns = enthalpy.shape
    targets = columns // width
    orders = stage_orders(nx, ny)
    f32 = jnp.float32
    total = nx * ny * targets
    given = (
        ocean_temp.reshape(cells, ci),
        ocean_salt.reshape(cells, ci),
        wet_mask.reshape(cells, ci),
        vertical_mix,
        friction,
        pressure,
        block_owner.reshape(1, blocks),
        block_target.reshape(1, blocks),
        pair_weight,
        transition_layer.reshape(targets, width),
        surface_enthalpy.reshape(targets, width),
        enthalpy,
        pair_column,
        column_area.reshape(targets, width),
    )
    results = (
        jax.ShapeDtypeStruct((cells, ci), f32),
        jax.ShapeDtypeStruct((cells, ci), f32),
        jax.ShapeDtypeStruct((layers, columns), f32),
        jax.ShapeDtypeStruct((targets, width), f32),
    )
    top_cells = 2 * CHUNK * cj
    scratch = [pltpu.VMEM(leaf.shape, leaf.dtype) for leaf in given]
    scratch += [pltpu.VMEM(leaf.shape, leaf.dtype) for leaf in results]
    scratch += [pltpu.SemaphoreType.DMA((len(given),)), pltpu.SemaphoreType.DMA((4,))]
    scratch += [
        pltpu.VMEM((cells + 2 * cj, ci), f32),
        pltpu.VMEM((4, cells, ci), f32),
        pltpu.VMEM((2, cells + 2 * cj, ci), f32),
        pltpu.VMEM((3, cells, ci), f32),
        pltpu.VMEM((2, cells, ci), f32),
        pltpu.VMEM((3, top_cells, ci), f32),
        pltpu.VMEM((2, top_cells, ci), f32),
        pltpu.VMEM((targets, width), f32),
        pltpu.VMEM((2, 3, levels, ci), f32),
        pltpu.VMEM((2, 3, levels, ci), f32),
        pltpu.VMEM((2, 8, cells), f32),
        pltpu.VMEM((2, 8, cells), f32),
        pltpu.VMEM((2, 2, levels, ci), f32),
        pltpu.VMEM((2, 2, levels, ci), f32),
        pltpu.VMEM((2, 8, cells), f32),
        pltpu.VMEM((2, 8, cells), f32),
        pltpu.VMEM((2, 3, CHUNK, ci), f32),
        pltpu.VMEM((2, 3, CHUNK, ci), f32),
        pltpu.VMEM((2, 8, top_cells), f32),
        pltpu.VMEM((2, 8, top_cells), f32),
        pltpu.VMEM((2, 2, CHUNK, ci), f32),
        pltpu.VMEM((2, 2, CHUNK, ci), f32),
        pltpu.VMEM((2, 8, top_cells), f32),
        pltpu.VMEM((2, 8, top_cells), f32),
        pltpu.VMEM((2, total, blocks), jnp.bfloat16),
        pltpu.VMEM((3, blocks, 2 * width), jnp.bfloat16),
        pltpu.VMEM((layers * targets, width), f32),
        pltpu.VMEM((layers * targets, width), f32),
    ]
    for order in (orders[0], orders[1], orders[0]):
        rows = live_rows(order, total)
        scratch += [pltpu.VMEM((n, width), f32) for n in rows]
        scratch += [
            pltpu.VMEM((radix - 1, n, width), f32)
            for (_, _, radix), n in zip(order, rows[1:])
        ]
        most = max(radix for _, _, radix in order) - 1
        scratch += [pltpu.SemaphoreType.DMA((len(order), most))] * 2
    scratch += [pltpu.SemaphoreType.DMA((4, 4))] * 2
    sizes = (nx, ny, levels, cj, ci, targets, layers)
    hbm = pl.BlockSpec(memory_space=pltpu.HBM)
    made = pl.pallas_call(
        functools.partial(kernel, sizes, orders),
        out_shape=results,
        in_specs=[hbm] * len(given),
        out_specs=(hbm,) * 4,
        scratch_shapes=scratch,
        compiler_params=pltpu.CompilerParams(
            collective_id=0, has_side_effects=True, vmem_limit_bytes=LIMIT
        ),
    )(*given)
    new_temp, new_salt, new_enthalpy, ice_melt = pl.pallas_call(
        store,
        out_shape=results,
        in_specs=[hbm] * 4,
        out_specs=(hbm,) * 4,
        scratch_shapes=[pltpu.SemaphoreType.DMA((4,))],
        compiler_params=pltpu.CompilerParams(vmem_limit_bytes=LIMIT),
    )(*made)
    return (
        new_temp.reshape(levels, cj, ci),
        new_salt.reshape(levels, cj, ci),
        new_enthalpy,
        ice_melt.reshape(columns),
    )


def solution(mesh):
    return jax.shard_map(
        functools.partial(local, mesh.shape["gx"], mesh.shape["gy"]),
        mesh=mesh,
        in_specs=(
            P(None, "gy", "gx"),
            P(None, "gy", "gx"),
            P(None, "gy", "gx"),
            P("gy", "gx"),
            P("gy", "gx"),
            P("gy", "gx"),
            P(("gx", "gy"), None),
            P(("gx", "gy"), None),
            P(("gx", "gy"), None),
            P(("gx", "gy")),
            P(None, ("gx", "gy")),
            P(("gx", "gy")),
            P(("gx", "gy")),
            P(("gx", "gy")),
        ),
        out_specs=(
            P(None, "gy", "gx"),
            P(None, "gy", "gx"),
            P(None, ("gx", "gy")),
            P(("gx", "gy")),
        ),
        check_vma=False,
    )
```

```python
import functools

import jax
import jax.numpy as jnp
from jax import lax
from jax.experimental import pallas as pl
from jax.experimental.pallas import tpu as pltpu
from jax.sharding import PartitionSpec as P

mixing_rate = 0.2
liquidus_slope = -0.0573
liquidus_base = 0.0832
liquidus_depth = -0.000753
latent_ratio = 4.0
salt_ratio = 35.0
relax_rate = 0.1
cold_rate = 2.0
temperate_rate = 0.2

MESH = pl.DeviceIdType.MESH
CHUNK = 8
PARTS = 2
LIMIT = 62 * 1024 * 1024


def shelf_melt(surface_temp, surface_salt, friction, pressure, wet_top):
    heat_gain = jnp.where(wet_top > 0, friction, 1.0)
    salt_safe = jnp.where(wet_top > 0, surface_salt, 34.0)
    salt_gain = heat_gain / salt_ratio
    curvature = heat_gain * liquidus_slope
    linear = (
        heat_gain * (surface_temp - liquidus_base - liquidus_depth * pressure)
        + latent_ratio * salt_gain
    )
    constant = latent_ratio * salt_gain * salt_safe
    boundary_salt = (
        2.0 * constant / (linear + jnp.sqrt(linear * linear - 4.0 * curvature * constant))
    )
    boundary_temp = liquidus_slope * boundary_salt + liquidus_base + liquidus_depth * pressure
    heat_flux = heat_gain * (surface_temp - boundary_temp) * wet_top
    salt_flux = salt_gain * (salt_safe - boundary_salt) * wet_top
    return (heat_flux, salt_flux, boundary_temp * wet_top)


def digits(axis, size):
    found = []
    base = 1
    while size > 1:
        radix = next(p for p in range(2, size + 1) if size % p == 0)
        if axis == "gx" and size == 4:
            radix = size
        found.append((axis, base, radix))
        base *= radix
        size //= radix
    return found


def stage_orders(nx, ny):
    gy = digits("gy", ny)
    gx = digits("gx", nx)
    first = gy + gx
    second = gy[:1] + gx[:1] + gy[1:] + gx[1:]
    return (first, second)


def slot_of(owner, order, ny):
    coord = {"gx": owner // ny, "gy": owner % ny}
    place = jnp.zeros_like(owner)
    for axis, base, radix in order:
        place = place * radix + (coord[axis] // base) % radix
    return place


def live_rows(order, total):
    rows = [total]
    for _, _, radix in order:
        rows.append(rows[-1] // radix)
    return rows


def split_two(value):
    high = value.astype(jnp.bfloat16)
    low = (value - high.astype(jnp.float32)).astype(jnp.bfloat16)
    return high, low


def kernel(sizes, orders, *refs):
    nx, ny, levels, cj, ci, targets, layers = sizes
    refs = list(refs)

    def take(count):
        out = refs[:count]
        del refs[:count]
        return out

    given = take(14)
    results = take(4)
    held = take(14)
    (out_temp, out_salt, out_enth, out_melt) = made = take(4)
    (load_sem, save_sem) = take(2)
    saves = [
        pltpu.make_async_copy(src, dst, save_sem.at[i])
        for i, (src, dst) in enumerate(zip(made, results))
    ]
    loads = [
        pltpu.make_async_copy(src, dst, load_sem.at[i])
        for i, (src, dst) in enumerate(zip(given, held))
    ]
    for load in loads:
        load.start()
    (temp, salt, wet, vmix, fric, pres, owner, target, pw, trans, surf, enth, pcol, area) = held
    (wetp, coef, mid, edge, first) = take(5)
    (edge_top, first_top, last_layer) = take(3)
    (row_send, row_recv, col_send, col_recv) = take(4)
    (row_send2, row_recv2, col_send2, col_recv2) = take(4)
    (row_top, row_top_in, col_top, col_top_in) = take(4)
    (row_top2, row_top_in2, col_top2, col_top_in2) = take(4)
    (hot, pay, ratios, values) = take(4)
    chains = []
    for order in (orders[0], orders[1], orders[0]) * PARTS:
        live = take(len(order) + 1)
        got = take(len(order))
        send_sem, recv_sem = take(2)
        chains.append((order, live, got, send_sem, recv_sem))
    (halo_send, halo_recv) = take(2)

    gx = lax.axis_index("gx")
    gy = lax.axis_index("gy")
    coord = {"gx": gx, "gy": gy}
    span = cj * CHUNK
    chunks = levels // CHUNK
    cells = levels * cj
    blocks = pcol.shape[0]
    width = pcol.shape[1]

    sides = (
        (gy > 0, {"gy": gy - 1}),
        (gy < ny - 1, {"gy": gy + 1}),
        (gx > 0, {"gx": gx - 1}),
        (gx < nx - 1, {"gx": gx + 1}),
    )

    for buf in (row_recv, row_recv2, row_top_in, row_top_in2):
        for side in range(2):
            @pl.when(jnp.logical_not(sides[side][0]))
            def _():
                buf[side] = jnp.zeros(buf.shape[1:], jnp.float32)
    for buf in (col_recv, col_recv2, col_top_in, col_top_in2):
        for side in range(2):
            @pl.when(jnp.logical_not(sides[2 + side][0]))
            def _():
                buf[side] = jnp.zeros(buf.shape[1:], jnp.float32)

    barrier = pltpu.get_barrier_semaphore()
    partners = 0
    for there, device in sides:
        @pl.when(there)
        def _():
            pl.semaphore_signal(barrier, inc=1, device_id=device, device_id_type=MESH)
        partners = partners + there.astype(jnp.int32)
    for axis, base, radix in orders[0]:
        mine = (coord[axis] // base) % radix
        for j in range(1, radix):
            peer = {axis: coord[axis] + ((mine + j) % radix - mine) * base}
            pl.semaphore_signal(barrier, inc=1, device_id=peer, device_id_type=MESH)
            partners = partners + 1

    zeros_pad = jnp.zeros((cj, ci), jnp.float32)
    wetp[pl.ds(0, cj), :] = zeros_pad
    wetp[pl.ds(cj + cells, cj), :] = zeros_pad
    for q in range(2):
        mid[q, pl.ds(0, cj), :] = zeros_pad
        mid[q, pl.ds(cj + cells, cj), :] = zeros_pad

    def pack(q, source, offset, rows, cols):
        count = rows.shape[2]
        rows[0, q] = source[pl.ds(offset, count, stride=cj), :]
        rows[1, q] = source[pl.ds(offset + cj - 1, count, stride=cj), :]
        turned = source[pl.ds(offset, cols.shape[2]), :].T
        cols[0, pl.ds(q, 1), :] = turned[0:1]
        cols[1, pl.ds(q, 1), :] = turned[ci - 1 : ci]

    for cols in (col_send, col_send2, col_top, col_top2):
        cols[...] = jnp.zeros(cols.shape, jnp.float32)
    first_top[...] = jnp.zeros(first_top.shape, jnp.float32)
    for load in loads[:3]:
        load.wait()
    wetp[pl.ds(cj, cells), :] = wet[...].astype(jnp.float32)

    def pack_all(rows, cols):
        pack(0, temp, 0, rows, cols)
        pack(1, salt, 0, rows, cols)
        pack(2, wetp, cj, rows, cols)

    pack_all(row_top, col_top)
    pl.semaphore_wait(barrier, partners)

    def halo(step, rows, rows_in, cols, cols_in):
        copies = []
        for side, (there, device) in enumerate(sides):
            src, dst = (rows, rows_in) if side < 2 else (cols, cols_in)
            copies.append(
                pltpu.make_async_remote_copy(
                    src_ref=src.at[side % 2],
                    dst_ref=dst.at[1 - side % 2],
                    send_sem=halo_send.at[step, side],
                    recv_sem=halo_recv.at[step, side - side % 2 + 1 - side % 2],
                    device_id=device,
                    device_id_type=MESH,
                )
            )
        return copies

    def halo_start(copies):
        for (there, _), copy in zip(sides, copies):
            @pl.when(there)
            def _():
                copy.start()

    def halo_wait(copies):
        for side, (there, _) in enumerate(sides):
            opposite = copies[side - side % 2 + 1 - side % 2]

            @pl.when(there)
            def _():
                opposite.wait_recv()

    def halo_done(copies):
        for (there, _), copy in zip(sides, copies):
            @pl.when(there)
            def _():
                copy.wait_send()

    halo_top1 = halo(2, row_top, row_top_in, col_top, col_top_in)
    halo_start(halo_top1)
    pack_all(row_send, col_send)
    halo1 = halo(0, row_send, row_recv, col_send, col_recv)
    halo_start(halo1)

    def make_copies(chain, stage):
        order, live, got, send_sem, recv_sem = chain
        axis, base, radix = order[stage]
        rows = live[stage + 1].shape[0]
        mine = (coord[axis] // base) % radix
        copies = []
        for j in range(1, radix):
            digit = (mine + j) % radix
            copies.append(
                pltpu.make_async_remote_copy(
                    src_ref=live[stage].at[pl.ds(digit * rows, rows)],
                    dst_ref=got[stage].at[j - 1],
                    send_sem=send_sem.at[stage, j - 1],
                    recv_sem=recv_sem.at[stage, j - 1],
                    device_id={axis: coord[axis] + (digit - mine) * base},
                    device_id_type=MESH,
                )
            )
        return copies

    def start_stage(chain, stage):
        for copy in make_copies(chain, stage):
            copy.start()

    def end_stage(chain, stage):
        order, live, got, _, _ = chain
        axis, base, radix = order[stage]
        rows = live[stage + 1].shape[0]
        mine = (coord[axis] // base) % radix
        total = live[stage][pl.ds(pl.multiple_of(mine * rows, rows), rows), :]
        for copy in make_copies(chain, stage):
            copy.wait_recv()
        for j in range(1, radix):
            total = total + got[stage][j - 1]
        live[stage + 1][...] = total
        if stage + 1 < len(order):
            start_stage(chain, stage + 1)

    def drain(chain):
        for stage in range(len(chain[0])):
            for copy in make_copies(chain, stage):
                copy.wait_send()

    part_rows = chains[0][1][0].shape[0]
    seg_total = part_rows * PARTS
    share_rows = targets // PARTS
    hot_rows = min(256, part_rows)

    def build_hot(which):
        place = target[...]
        part = place // share_rows
        seg = slot_of(owner[...], orders[which], ny) * share_rows + place - part * share_rows
        seg = part * part_rows + seg

        def body(i, carry):
            start = pl.multiple_of(i * hot_rows, hot_rows)
            row = lax.broadcasted_iota(jnp.int32, (hot_rows, blocks), 0) + start
            hit = (row == seg).astype(jnp.float32)
            hot[which, pl.ds(start, hot_rows), :] = hit.astype(jnp.bfloat16)
            return carry

        lax.fori_loop(0, seg_total // hot_rows, body, 0)

    def sum_blocks(which, slot, part):
        goal = chains[part * 3 + slot][1][0]

        def body(i, carry):
            start = pl.multiple_of(i * hot_rows, hot_rows)
            both = jnp.dot(
                hot[which, pl.ds(pl.multiple_of(part * part_rows + start, hot_rows), hot_rows), :],
                pay[slot],
                preferred_element_type=jnp.float32,
            )
            goal[pl.ds(start, hot_rows), :] = both[:, :width] + both[:, width:]
            return carry

        lax.fori_loop(0, part_rows // hot_rows, body, 0)
        start_stage(chains[part * 3 + slot], 0)

    def end_stages(slot, stage):
        for part in range(PARTS):
            end_stage(chains[part * 3 + slot], stage)

    for load in loads[6:9]:
        load.wait()
    build_hot(0)
    high, low = split_two(pw[...])
    pay[2, :, pl.ds(0, width)] = high
    pay[2, :, pl.ds(width, width)] = low
    for part in range(PARTS):
        sum_blocks(0, 2, part)
    for load in loads[3:6]:
        load.wait()

    lane = lax.broadcasted_iota(jnp.int32, (CHUNK, cj, ci), 2)
    row = lax.broadcasted_iota(jnp.int32, (CHUNK, cj, ci), 1)

    def spread_edge(q, cols_in, edge):
        turned = lax.broadcasted_iota(jnp.int32, (ci, cols_in.shape[2]), 0)
        both = jnp.where(turned == 0, cols_in[0, pl.ds(q, 1), :], cols_in[1, pl.ds(q, 1), :])
        edge[q] = both.T

    def around(x, q, c, rows_in, edge):
        start = pl.multiple_of(c * span, span)
        level = pl.ds(pl.multiple_of(c * CHUNK, CHUNK), CHUNK)
        side = edge[q, pl.ds(start, span), :].reshape(CHUNK, cj, ci)
        west = jnp.where(lane == 0, side, pltpu.roll(x, 1, 2))
        east = jnp.where(lane == ci - 1, side, pltpu.roll(x, ci - 1, 2))
        north = jnp.where(row == 0, rows_in[0, q, level, :][:, None, :], pltpu.roll(x, 1, 1))
        south = jnp.where(
            row == cj - 1, rows_in[1, q, level, :][:, None, :], pltpu.roll(x, cj - 1, 1)
        )
        return west, east, north, south

    def couple(rows_in, edge, c):
        start = pl.multiple_of(c * span, span)
        x = wetp[pl.ds(pl.multiple_of(cj + start, cj), span), :].reshape(CHUNK, cj, ci)
        for n, beside in enumerate(around(x, 2, c, rows_in, edge)):
            coef[n, pl.ds(start, span), :] = (mixing_rate * (x * beside)).reshape(span, ci)

    def spread(sources, rows_in, edge, c):
        start = pl.multiple_of(c * span, span)
        weights = [coef[n, pl.ds(start, span), :].reshape(CHUNK, cj, ci) for n in range(4)]
        for q in range(2):
            x = sources[q][pl.ds(start, span), :].reshape(CHUNK, cj, ci)
            total = x
            for weight, beside in zip(weights, around(x, q, c, rows_in, edge)):
                total = total + weight * (beside - x)
            mid[q, pl.ds(pl.multiple_of(cj + start, cj), span), :] = total.reshape(span, ci)

    def mix(c, targets_of):
        start = pl.multiple_of(c * span, span)
        up = pl.ds(start, span)
        here = pl.ds(pl.multiple_of(start + cj, cj), span)
        down = pl.ds(pl.multiple_of(start + 2 * cj, cj), span)
        rate = jnp.broadcast_to(vmix[...][None], (CHUNK, cj, ci)).reshape(span, ci)
        wet_here = rate * wetp[here, :]
        link_up = wet_here * wetp[up, :]
        link_down = wet_here * wetp[down, :]
        for q in range(2):
            x = mid[q, here, :]
            targets_of[q][pl.ds(start, span), :] = (
                x + link_down * (mid[q, down, :] - x) - link_up * (x - mid[q, up, :])
            )

    wet_top = wetp[pl.ds(cj, cj), :]

    def surface():
        link = vmix[...] * wet_top * wetp[pl.ds(2 * cj, cj), :]
        top = []
        for q in range(2):
            x = mid[q, pl.ds(cj, cj), :]
            top.append(x + link * (mid[q, pl.ds(2 * cj, cj), :] - x))
        heat, saltf, base_temp = shelf_melt(top[0], top[1], fric[...], pres[...], wet_top)
        return (
            top[0] - relax_rate * heat,
            top[1] - relax_rate * saltf,
            heat / latent_ratio,
            base_temp,
        )

    def loop(low_c, high_c, body):
        def wrapped(c, carry):
            body(c)
            return carry

        lax.fori_loop(low_c, high_c, wrapped, 0)

    halo_wait(halo_top1)
    for q in range(3):
        spread_edge(q, col_top_in, edge_top)
    couple(row_top_in, edge_top, 0)
    spread((temp, salt), row_top_in, edge_top, 0)
    mix(0, (first_top.at[0], first_top.at[1]))
    top_temp, top_salt, melt_one, base_one = surface()
    first_top[0, pl.ds(0, cj), :] = top_temp
    first_top[1, pl.ds(0, cj), :] = top_salt
    for q in range(2):
        pack(q, first_top.at[q], 0, row_top2, col_top2)
    halo_top2 = halo(3, row_top2, row_top_in2, col_top2, col_top_in2)
    halo_start(halo_top2)

    build_hot(1)
    end_stages(2, 0)
    for load in loads[9:12]:
        load.wait()
    groups = enth.shape[1] // width
    for g in range(groups):
        values[pl.ds(g * layers, layers), :] = enth[:, g * width : (g + 1) * width]

    def rate_of(k):
        return jnp.where(k < trans[...], cold_rate, temperate_rate).astype(jnp.float32)

    def layer(k):
        return pl.ds(k, groups, stride=layers)

    def eliminate(k, carry):
        ratio, value, rate, inner_up = carry
        rate_next = rate_of(k + 1)
        inner = 0.5 * (rate + rate_next)
        pivot = 1.0 / (1.0 + inner_up + inner + inner_up * ratio)
        value = (values[layer(k), :] + inner_up * value) * pivot
        ratio = -inner * pivot
        values[layer(k), :] = value
        ratios[layer(k), :] = ratio
        return ratio, value, rate_next, inner

    last = layers - 1

    halo_wait(halo_top2)
    for q in range(2):
        spread_edge(q, col_top_in2, edge_top)
    spread((first_top.at[0], first_top.at[1]), row_top_in2, edge_top, 0)
    new_top_temp, new_top_salt, melt_two, base_two = surface()
    mean_melt = 0.5 * (melt_one + melt_two)
    mean_base = 0.5 * (base_one + base_two)
    for load in loads[12:]:
        load.wait()

    batch = 64

    def pairs(i, carry):
        at = pl.ds(pl.multiple_of(i * batch, batch), batch)
        place = pcol[at, :]
        place_row = place // ci
        place_col = place - place_row * ci
        weight = pw[at, :]
        for slot, table in ((0, mean_melt), (1, mean_base)):
            found = jnp.zeros((batch, width), jnp.float32)
            for r in range(cj):
                line = jnp.broadcast_to(table[r : r + 1], (batch, ci))
                there = jnp.take_along_axis(
                    line, place_col, axis=1, mode="promise_in_bounds"
                )
                found = jnp.where(place_row == r, there, found)
            high, low = split_two(weight * found)
            pay[slot, at, pl.ds(0, width)] = high
            pay[slot, at, pl.ds(width, width)] = low
        return carry

    lax.fori_loop(0, blocks // batch, pairs, 0)
    for part in range(PARTS):
        for slot in range(2):
            sum_blocks(slot, slot, part)

    halo2 = halo(1, row_send2, row_recv2, col_send2, col_recv2)

    def first_couple():
        halo_wait(halo1)
        for q in range(3):
            spread_edge(q, col_recv, edge)
        loop(0, chunks, functools.partial(couple, row_recv, edge))

    def first_spread():
        loop(0, chunks, functools.partial(spread, (temp, salt), row_recv, edge))

    def first_mix():
        loop(0, chunks, lambda c: mix(c, (first.at[0], first.at[1])))
        first[0, pl.ds(0, cj), :] = top_temp
        first[1, pl.ds(0, cj), :] = top_salt
        for q in range(2):
            pack(q, first.at[q], 0, row_send2, col_send2)
        halo_start(halo2)

    def second_step():
        halo_wait(halo2)
        for q in range(2):
            spread_edge(q, col_recv2, edge)
        sources = (first.at[0], first.at[1])
        loop(0, chunks, functools.partial(spread, sources, row_recv2, edge))
        loop(0, chunks, lambda c: mix(c, (out_temp, out_salt)))
        out_temp[pl.ds(0, cj), :] = new_top_temp
        out_salt[pl.ds(0, cj), :] = new_top_salt
        saves[0].start()
        saves[1].start()

    middle = 1 + (last - 1) // 2

    def forward_first():
        rate_top = rate_of(0)
        rate_next = rate_of(1)
        inner = 0.5 * (rate_top + rate_next)
        pivot = 1.0 / (1.0 + rate_top + inner)
        value = (values[layer(0), :] + rate_top * surf[...]) * pivot
        ratio = -inner * pivot
        values[layer(0), :] = value
        ratios[layer(0), :] = ratio
        return lax.fori_loop(1, middle, eliminate, (ratio, value, rate_next, inner))

    def forward_rest(state):
        return lax.fori_loop(middle, last, eliminate, state)

    def back_terms(state):
        ratio_end, value_end, _, _ = state
        ratios[layer(last - 1), :] = -ratio_end

        def body(n, carry):
            level, slope = carry
            k = last - 2 - n
            ratio = ratios[layer(k), :]
            level = values[layer(k), :] - ratio * level
            slope = -ratio * slope
            values[layer(k), :] = level
            ratios[layer(k), :] = slope
            return level, slope

        lax.fori_loop(0, last - 1, body, (value_end, -ratio_end))
        last_side = values[layer(last), :]
        values[layer(last), :] = jnp.zeros((groups, width), jnp.float32)
        ratios[layer(last), :] = jnp.ones((groups, width), jnp.float32)
        return last_side

    stages = len(orders[0])

    def advance(stage):
        for part in range(PARTS):
            for slot in range(2):
                end_stage(chains[part * 3 + slot], stage)
        if stage + 1 < stages:
            end_stages(2, stage + 1)

    first_couple()
    advance(0)
    first_spread()
    first_mix()
    state = forward_first()
    if stages > 1:
        advance(1)
    state = forward_rest(state)
    if stages > 2:
        advance(2)
    last_side = back_terms(state)
    second_step()
    for stage in range(3, stages):
        advance(stage)
    ratio_end, value_end, _, inner_end = state

    share = 1.0 / area[...]
    sums = [
        jnp.concatenate([chains[part * 3 + slot][1][-1][...] for part in range(PARTS)], axis=0)
        for slot in range(3)
    ]
    melt_sum = sums[0] * share
    base_sum = sums[1] * share
    cover_sum = sums[2] * share
    out_melt[...] = melt_sum
    pivot = 1.0 / (1.0 + inner_end + cover_sum + inner_end * ratio_end)
    last_layer[...] = (last_side + base_sum + inner_end * value_end) * pivot
    for g in range(groups):
        rows = pl.ds(g * layers, layers)
        solved = values[rows, :] + ratios[rows, :] * last_layer[pl.ds(g, 1), :]
        out_enth[:, g * width : (g + 1) * width] = solved
    saves[2].start()
    saves[3].start()

    halo_done(halo_top1)
    halo_done(halo_top2)
    halo_done(halo1)
    halo_done(halo2)
    for chain in chains:
        drain(chain)
    for save in saves:
        save.wait()


def store(*refs):
    count = len(refs) // 3
    sems = refs[3 * count]
    inward = []
    outward = []
    for i in range(count):
        src, dst, held = refs[i], refs[count + i], refs[2 * count + i]
        inward.append(pltpu.make_async_copy(src, held, sems.at[0, i]))
        outward.append(pltpu.make_async_copy(held, dst, sems.at[1, i]))
    for copy in inward:
        copy.start()
    for first, then in zip(inward, outward):
        first.wait()
        then.start()
    for copy in outward:
        copy.wait()


def local(
    nx,
    ny,
    ocean_temp,
    ocean_salt,
    wet_mask,
    vertical_mix,
    friction,
    pressure,
    pair_column,
    pair_weight,
    block_owner,
    block_target,
    enthalpy,
    surface_enthalpy,
    transition_layer,
    column_area,
):
    levels, cj, ci = wet_mask.shape
    cells = levels * cj
    blocks, width = pair_column.shape
    layers, columns = enthalpy.shape
    targets = columns // width
    orders = stage_orders(nx, ny)
    f32 = jnp.float32
    total = nx * ny * targets
    given = (
        ocean_temp.reshape(cells, ci),
        ocean_salt.reshape(cells, ci),
        wet_mask.reshape(cells, ci),
        vertical_mix,
        friction,
        pressure,
        block_owner.reshape(1, blocks),
        block_target.reshape(1, blocks),
        pair_weight,
        transition_layer.reshape(targets, width),
        surface_enthalpy.reshape(targets, width),
        enthalpy,
        pair_column,
        column_area.reshape(targets, width),
    )
    results = (
        jax.ShapeDtypeStruct((cells, ci), f32),
        jax.ShapeDtypeStruct((cells, ci), f32),
        jax.ShapeDtypeStruct((layers, columns), f32),
        jax.ShapeDtypeStruct((targets, width), f32),
    )
    top_cells = 2 * CHUNK * cj
    scratch = [pltpu.VMEM(leaf.shape, leaf.dtype) for leaf in given]
    scratch += [pltpu.VMEM(leaf.shape, leaf.dtype) for leaf in results]
    scratch += [pltpu.SemaphoreType.DMA((len(given),)), pltpu.SemaphoreType.DMA((4,))]
    scratch += [
        pltpu.VMEM((cells + 2 * cj, ci), f32),
        pltpu.VMEM((4, cells, ci), f32),
        pltpu.VMEM((2, cells + 2 * cj, ci), f32),
        pltpu.VMEM((3, cells, ci), f32),
        pltpu.VMEM((2, cells, ci), f32),
        pltpu.VMEM((3, top_cells, ci), f32),
        pltpu.VMEM((2, top_cells, ci), f32),
        pltpu.VMEM((targets, width), f32),
        pltpu.VMEM((2, 3, levels, ci), f32),
        pltpu.VMEM((2, 3, levels, ci), f32),
        pltpu.VMEM((2, 8, cells), f32),
        pltpu.VMEM((2, 8, cells), f32),
        pltpu.VMEM((2, 2, levels, ci), f32),
        pltpu.VMEM((2, 2, levels, ci), f32),
        pltpu.VMEM((2, 8, cells), f32),
        pltpu.VMEM((2, 8, cells), f32),
        pltpu.VMEM((2, 3, CHUNK, ci), f32),
        pltpu.VMEM((2, 3, CHUNK, ci), f32),
        pltpu.VMEM((2, 8, top_cells), f32),
        pltpu.VMEM((2, 8, top_cells), f32),
        pltpu.VMEM((2, 2, CHUNK, ci), f32),
        pltpu.VMEM((2, 2, CHUNK, ci), f32),
        pltpu.VMEM((2, 8, top_cells), f32),
        pltpu.VMEM((2, 8, top_cells), f32),
        pltpu.VMEM((2, total, blocks), jnp.bfloat16),
        pltpu.VMEM((3, blocks, 2 * width), jnp.bfloat16),
        pltpu.VMEM((layers * targets, width), f32),
        pltpu.VMEM((layers * targets, width), f32),
    ]
    for order in (orders[0], orders[1], orders[0]) * PARTS:
        rows = live_rows(order, total // PARTS)
        scratch += [pltpu.VMEM((n, width), f32) for n in rows]
        scratch += [
            pltpu.VMEM((radix - 1, n, width), f32)
            for (_, _, radix), n in zip(order, rows[1:])
        ]
        most = max(radix for _, _, radix in order) - 1
        scratch += [pltpu.SemaphoreType.DMA((len(order), most))] * 2
    scratch += [pltpu.SemaphoreType.DMA((4, 4))] * 2
    sizes = (nx, ny, levels, cj, ci, targets, layers)
    hbm = pl.BlockSpec(memory_space=pltpu.HBM)
    made = pl.pallas_call(
        functools.partial(kernel, sizes, orders),
        out_shape=results,
        in_specs=[hbm] * len(given),
        out_specs=(hbm,) * 4,
        scratch_shapes=scratch,
        compiler_params=pltpu.CompilerParams(
            collective_id=0, has_side_effects=True, vmem_limit_bytes=LIMIT
        ),
    )(*given)
    new_temp, new_salt, new_enthalpy, ice_melt = pl.pallas_call(
        store,
        out_shape=results,
        in_specs=[hbm] * 4,
        out_specs=(hbm,) * 4,
        scratch_shapes=[pltpu.VMEM(leaf.shape, leaf.dtype) for leaf in results]
        + [pltpu.SemaphoreType.DMA((2, 4))],
        compiler_params=pltpu.CompilerParams(vmem_limit_bytes=LIMIT),
    )(*made)
    return (
        new_temp.reshape(levels, cj, ci),
        new_salt.reshape(levels, cj, ci),
        new_enthalpy,
        ice_melt.reshape(columns),
    )


def solution(mesh):
    return jax.shard_map(
        functools.partial(local, mesh.shape["gx"], mesh.shape["gy"]),
        mesh=mesh,
        in_specs=(
            P(None, "gy", "gx"),
            P(None, "gy", "gx"),
            P(None, "gy", "gx"),
            P("gy", "gx"),
            P("gy", "gx"),
            P("gy", "gx"),
            P(("gx", "gy"), None),
            P(("gx", "gy"), None),
            P(("gx", "gy"), None),
            P(("gx", "gy")),
            P(None, ("gx", "gy")),
            P(("gx", "gy")),
            P(("gx", "gy")),
            P(("gx", "gy")),
        ),
        out_specs=(
            P(None, "gy", "gx"),
            P(None, "gy", "gx"),
            P(None, ("gx", "gy")),
            P(("gx", "gy")),
        ),
        check_vma=False,
    )
```

```python
import functools

import jax
import jax.numpy as jnp
from jax import lax
from jax.experimental import pallas as pl
from jax.experimental.pallas import tpu as pltpu
from jax.sharding import PartitionSpec as P

mixing_rate = 0.2
liquidus_slope = -0.0573
liquidus_base = 0.0832
liquidus_depth = -0.000753
latent_ratio = 4.0
salt_ratio = 35.0
relax_rate = 0.1
cold_rate = 2.0
temperate_rate = 0.2

MESH = pl.DeviceIdType.MESH
CHUNK = 8
PARTS = 2
LIMIT = 62 * 1024 * 1024


def shelf_melt(surface_temp, surface_salt, friction, pressure, wet_top):
    heat_gain = jnp.where(wet_top > 0, friction, 1.0)
    salt_safe = jnp.where(wet_top > 0, surface_salt, 34.0)
    salt_gain = heat_gain / salt_ratio
    curvature = heat_gain * liquidus_slope
    linear = (
        heat_gain * (surface_temp - liquidus_base - liquidus_depth * pressure)
        + latent_ratio * salt_gain
    )
    constant = latent_ratio * salt_gain * salt_safe
    boundary_salt = (
        2.0 * constant / (linear + jnp.sqrt(linear * linear - 4.0 * curvature * constant))
    )
    boundary_temp = liquidus_slope * boundary_salt + liquidus_base + liquidus_depth * pressure
    heat_flux = heat_gain * (surface_temp - boundary_temp) * wet_top
    salt_flux = salt_gain * (salt_safe - boundary_salt) * wet_top
    return (heat_flux, salt_flux, boundary_temp * wet_top)


def quotient(value, size):
    if size & (size - 1):
        return value // size
    return lax.shift_right_logical(value, size.bit_length() - 1)


def remainder(value, size):
    return value - quotient(value, size) * size if size & (size - 1) else value & (size - 1)


def digits(axis, size):
    found = []
    base = 1
    while size > 1:
        radix = next(p for p in range(2, size + 1) if size % p == 0)
        if axis == "gx" and size == 4:
            radix = size
        found.append((axis, base, radix))
        base *= radix
        size //= radix
    return found


def stage_orders(nx, ny):
    gy = digits("gy", ny)
    gx = digits("gx", nx)
    first = gy + gx
    second = gy[:1] + gx[:1] + gy[1:] + gx[1:]
    return (first, second)


def slot_of(owner, order, ny):
    coord = {"gx": quotient(owner, ny), "gy": remainder(owner, ny)}
    place = jnp.zeros_like(owner)
    for axis, base, radix in order:
        place = place * radix + remainder(quotient(coord[axis], base), radix)
    return place


def live_rows(order, total):
    rows = [total]
    for _, _, radix in order:
        rows.append(rows[-1] // radix)
    return rows


def inverse(value):
    guess = pl.reciprocal(value, approx=True)
    guess = guess * (2.0 - value * guess)
    return guess * (2.0 - value * guess)


def split_two(value):
    high = value.astype(jnp.bfloat16)
    low = (value - high.astype(jnp.float32)).astype(jnp.bfloat16)
    return high, low


def kernel(sizes, orders, *refs):
    nx, ny, levels, cj, ci, targets, layers = sizes
    refs = list(refs)

    def take(count):
        out = refs[:count]
        del refs[:count]
        return out

    given = take(14)
    results = take(4)
    held = take(14)
    (out_temp, out_salt, out_enth, out_melt) = made = take(4)
    (load_sem, save_sem) = take(2)
    saves = [
        pltpu.make_async_copy(src, dst, save_sem.at[i])
        for i, (src, dst) in enumerate(zip(made, results))
    ]
    loads = [
        pltpu.make_async_copy(src, dst, load_sem.at[i])
        for i, (src, dst) in enumerate(zip(given, held))
    ]
    for load in loads:
        load.start()
    (temp, salt, wet, vmix, fric, pres, owner, target, pw, trans, surf, enth, pcol, area) = held
    (wetp, coef, mid, edge, first) = take(5)
    (edge_top, first_top, last_layer) = take(3)
    (row_send, row_recv, col_send, col_recv) = take(4)
    (row_send2, row_recv2, col_send2, col_recv2) = take(4)
    (row_top, row_top_in, col_top, col_top_in) = take(4)
    (row_top2, row_top_in2, col_top2, col_top_in2) = take(4)
    (hot, pay, ratios, values) = take(4)
    chains = []
    for order in (orders[0], orders[1], orders[0]) * PARTS:
        live = take(len(order) + 1)
        got = take(len(order))
        send_sem, recv_sem = take(2)
        chains.append((order, live, got, send_sem, recv_sem))
    (halo_send, halo_recv) = take(2)

    gx = lax.axis_index("gx")
    gy = lax.axis_index("gy")
    coord = {"gx": gx, "gy": gy}
    span = cj * CHUNK
    chunks = levels // CHUNK
    cells = levels * cj
    blocks = pcol.shape[0]
    width = pcol.shape[1]

    sides = (
        (gy > 0, {"gy": gy - 1}),
        (gy < ny - 1, {"gy": gy + 1}),
        (gx > 0, {"gx": gx - 1}),
        (gx < nx - 1, {"gx": gx + 1}),
    )

    for buf in (row_recv, row_recv2, row_top_in, row_top_in2):
        for side in range(2):
            @pl.when(jnp.logical_not(sides[side][0]))
            def _():
                buf[side] = jnp.zeros(buf.shape[1:], jnp.float32)
    for buf in (col_recv, col_recv2, col_top_in, col_top_in2):
        for side in range(2):
            @pl.when(jnp.logical_not(sides[2 + side][0]))
            def _():
                buf[side] = jnp.zeros(buf.shape[1:], jnp.float32)

    barrier = pltpu.get_barrier_semaphore()
    partners = 0
    for there, device in sides:
        @pl.when(there)
        def _():
            pl.semaphore_signal(barrier, inc=1, device_id=device, device_id_type=MESH)
        partners = partners + there.astype(jnp.int32)
    for axis, base, radix in orders[0]:
        mine = (coord[axis] // base) % radix
        for j in range(1, radix):
            peer = {axis: coord[axis] + ((mine + j) % radix - mine) * base}
            pl.semaphore_signal(barrier, inc=1, device_id=peer, device_id_type=MESH)
            partners = partners + 1

    zeros_pad = jnp.zeros((cj, ci), jnp.float32)
    wetp[pl.ds(0, cj), :] = zeros_pad
    wetp[pl.ds(cj + cells, cj), :] = zeros_pad
    for q in range(2):
        mid[q, pl.ds(0, cj), :] = zeros_pad
        mid[q, pl.ds(cj + cells, cj), :] = zeros_pad

    def pack(q, source, offset, rows, cols):
        count = rows.shape[2]
        rows[0, q] = source[pl.ds(offset, count, stride=cj), :]
        rows[1, q] = source[pl.ds(offset + cj - 1, count, stride=cj), :]
        turned = source[pl.ds(offset, cols.shape[2]), :].T
        cols[0, pl.ds(q, 1), :] = turned[0:1]
        cols[1, pl.ds(q, 1), :] = turned[ci - 1 : ci]

    for cols in (col_send, col_send2, col_top, col_top2):
        cols[...] = jnp.zeros(cols.shape, jnp.float32)
    first_top[...] = jnp.zeros(first_top.shape, jnp.float32)
    for load in loads[:3]:
        load.wait()
    wetp[pl.ds(cj, cells), :] = wet[...].astype(jnp.float32)

    def pack_all(rows, cols):
        pack(0, temp, 0, rows, cols)
        pack(1, salt, 0, rows, cols)
        pack(2, wetp, cj, rows, cols)

    pack_all(row_top, col_top)
    pl.semaphore_wait(barrier, partners)

    def halo(step, rows, rows_in, cols, cols_in):
        copies = []
        for side, (there, device) in enumerate(sides):
            src, dst = (rows, rows_in) if side < 2 else (cols, cols_in)
            copies.append(
                pltpu.make_async_remote_copy(
                    src_ref=src.at[side % 2],
                    dst_ref=dst.at[1 - side % 2],
                    send_sem=halo_send.at[step, side],
                    recv_sem=halo_recv.at[step, side - side % 2 + 1 - side % 2],
                    device_id=device,
                    device_id_type=MESH,
                )
            )
        return copies

    def halo_start(copies):
        for (there, _), copy in zip(sides, copies):
            @pl.when(there)
            def _():
                copy.start()

    def halo_wait(copies):
        for side, (there, _) in enumerate(sides):
            opposite = copies[side - side % 2 + 1 - side % 2]

            @pl.when(there)
            def _():
                opposite.wait_recv()

    def halo_done(copies):
        for (there, _), copy in zip(sides, copies):
            @pl.when(there)
            def _():
                copy.wait_send()

    halo_top1 = halo(2, row_top, row_top_in, col_top, col_top_in)
    halo_start(halo_top1)

    def make_copies(chain, stage):
        order, live, got, send_sem, recv_sem = chain
        axis, base, radix = order[stage]
        rows = live[stage + 1].shape[0]
        mine = (coord[axis] // base) % radix
        copies = []
        for j in range(1, radix):
            digit = (mine + j) % radix
            copies.append(
                pltpu.make_async_remote_copy(
                    src_ref=live[stage].at[pl.ds(digit * rows, rows)],
                    dst_ref=got[stage].at[j - 1],
                    send_sem=send_sem.at[stage, j - 1],
                    recv_sem=recv_sem.at[stage, j - 1],
                    device_id={axis: coord[axis] + (digit - mine) * base},
                    device_id_type=MESH,
                )
            )
        return copies

    def start_stage(chain, stage):
        for copy in make_copies(chain, stage):
            copy.start()

    def end_stage(chain, stage):
        order, live, got, _, _ = chain
        axis, base, radix = order[stage]
        rows = live[stage + 1].shape[0]
        mine = (coord[axis] // base) % radix
        total = live[stage][pl.ds(pl.multiple_of(mine * rows, rows), rows), :]
        for copy in make_copies(chain, stage):
            copy.wait_recv()
        for j in range(1, radix):
            total = total + got[stage][j - 1]
        live[stage + 1][...] = total
        if stage + 1 < len(order):
            start_stage(chain, stage + 1)

    def drain(chain, stages_done):
        for stage in stages_done:
            for copy in make_copies(chain, stage):
                copy.wait_send()

    part_rows = chains[0][1][0].shape[0]
    seg_total = part_rows * PARTS
    share_rows = targets // PARTS
    hot_rows = min(256, part_rows)

    def build_hot():
        place = target[...]
        seg = slot_of(owner[...], orders[0], ny) * share_rows + remainder(place, share_rows)
        seg = quotient(place, share_rows) * part_rows + seg

        def body(i, carry):
            start = pl.multiple_of(i * hot_rows, hot_rows)
            row = lax.broadcasted_iota(jnp.int32, (hot_rows, blocks), 0) + start
            hit = (row == seg).astype(jnp.float32)
            hot[pl.ds(start, hot_rows), :] = hit.astype(jnp.bfloat16)
            return carry

        lax.fori_loop(0, seg_total // hot_rows, body, 0)

    def placed(order):
        common = 0
        while common < len(order) and order[-1 - common] == orders[0][-1 - common]:
            common += 1
        run = share_rows
        for _, _, radix in order[len(order) - common :]:
            run *= radix
        head = orders[0][: len(order) - common]
        goals = []
        for n in range(part_rows // run):
            left = n
            at = {}
            for digit in reversed(head):
                at[digit] = left % digit[2]
                left //= digit[2]
            goal = 0
            for digit in order[: len(order) - common]:
                goal = goal * digit[2] + at[digit]
            goals.append(goal * run)
        return run, goals

    def sum_blocks(slot, part):
        order, live = chains[part * 3 + slot][:2]
        run, goals = placed(order)
        step = min(run, hot_rows)
        for start in range(0, part_rows, hot_rows):
            both = jnp.dot(
                hot[pl.ds(part * part_rows + start, hot_rows), :],
                pay[slot],
                preferred_element_type=jnp.float32,
            )
            both = both[:, :width] + both[:, width:]
            for piece in range(0, hot_rows, step):
                n, inside = divmod(start + piece, run)
                live[0][pl.ds(goals[n] + inside, step), :] = both[piece : piece + step]
        start_stage(chains[part * 3 + slot], 0)

    def end_stages(slot, stage):
        for part in range(PARTS):
            end_stage(chains[part * 3 + slot], stage)

    for load in loads[6:9]:
        load.wait()
    build_hot()
    high, low = split_two(pw[...])
    pay[2, :, pl.ds(0, width)] = high
    pay[2, :, pl.ds(width, width)] = low
    for part in range(PARTS):
        sum_blocks(2, part)
    for load in loads[3:6]:
        load.wait()

    lane = lax.broadcasted_iota(jnp.int32, (CHUNK, cj, ci), 2)
    row = lax.broadcasted_iota(jnp.int32, (CHUNK, cj, ci), 1)

    def spread_edge(q, cols_in, edge):
        turned = lax.broadcasted_iota(jnp.int32, (ci, cols_in.shape[2]), 0)
        both = jnp.where(turned == 0, cols_in[0, pl.ds(q, 1), :], cols_in[1, pl.ds(q, 1), :])
        edge[q] = both.T

    def around(x, q, c, rows_in, edge):
        start = pl.multiple_of(c * span, span)
        level = pl.ds(pl.multiple_of(c * CHUNK, CHUNK), CHUNK)
        side = edge[q, pl.ds(start, span), :].reshape(CHUNK, cj, ci)
        west = jnp.where(lane == 0, side, pltpu.roll(x, 1, 2))
        east = jnp.where(lane == ci - 1, side, pltpu.roll(x, ci - 1, 2))
        north = jnp.where(row == 0, rows_in[0, q, level, :][:, None, :], pltpu.roll(x, 1, 1))
        south = jnp.where(
            row == cj - 1, rows_in[1, q, level, :][:, None, :], pltpu.roll(x, cj - 1, 1)
        )
        return west, east, north, south

    def couple(rows_in, edge, c):
        start = pl.multiple_of(c * span, span)
        x = wetp[pl.ds(pl.multiple_of(cj + start, cj), span), :].reshape(CHUNK, cj, ci)
        for n, beside in enumerate(around(x, 2, c, rows_in, edge)):
            coef[n, pl.ds(start, span), :] = (mixing_rate * (x * beside)).reshape(span, ci)

    def spread(sources, rows_in, edge, c):
        start = pl.multiple_of(c * span, span)
        weights = [coef[n, pl.ds(start, span), :].reshape(CHUNK, cj, ci) for n in range(4)]
        for q in range(2):
            x = sources[q][pl.ds(start, span), :].reshape(CHUNK, cj, ci)
            total = x
            for weight, beside in zip(weights, around(x, q, c, rows_in, edge)):
                total = total + weight * (beside - x)
            mid[q, pl.ds(pl.multiple_of(cj + start, cj), span), :] = total.reshape(span, ci)

    def mix(c, targets_of):
        start = pl.multiple_of(c * span, span)
        up = pl.ds(start, span)
        here = pl.ds(pl.multiple_of(start + cj, cj), span)
        down = pl.ds(pl.multiple_of(start + 2 * cj, cj), span)
        rate = jnp.broadcast_to(vmix[...][None], (CHUNK, cj, ci)).reshape(span, ci)
        wet_here = rate * wetp[here, :]
        link_up = wet_here * wetp[up, :]
        link_down = wet_here * wetp[down, :]
        for q in range(2):
            x = mid[q, here, :]
            targets_of[q][pl.ds(start, span), :] = (
                x + link_down * (mid[q, down, :] - x) - link_up * (x - mid[q, up, :])
            )

    wet_top = wetp[pl.ds(cj, cj), :]

    def surface():
        link = vmix[...] * wet_top * wetp[pl.ds(2 * cj, cj), :]
        top = []
        for q in range(2):
            x = mid[q, pl.ds(cj, cj), :]
            top.append(x + link * (mid[q, pl.ds(2 * cj, cj), :] - x))
        heat, saltf, base_temp = shelf_melt(top[0], top[1], fric[...], pres[...], wet_top)
        return (
            top[0] - relax_rate * heat,
            top[1] - relax_rate * saltf,
            heat / latent_ratio,
            base_temp,
        )

    def loop(low_c, high_c, body):
        def wrapped(c, carry):
            body(c)
            return carry

        lax.fori_loop(low_c, high_c, wrapped, 0)

    halo_wait(halo_top1)
    for q in range(3):
        spread_edge(q, col_top_in, edge_top)
    couple(row_top_in, edge_top, 0)
    spread((temp, salt), row_top_in, edge_top, 0)
    mix(0, (first_top.at[0], first_top.at[1]))
    top_temp, top_salt, melt_one, base_one = surface()
    first_top[0, pl.ds(0, cj), :] = top_temp
    first_top[1, pl.ds(0, cj), :] = top_salt
    for q in range(2):
        pack(q, first_top.at[q], 0, row_top2, col_top2)
    halo_top2 = halo(3, row_top2, row_top_in2, col_top2, col_top_in2)
    halo_start(halo_top2)

    pack_all(row_send, col_send)
    halo1 = halo(0, row_send, row_recv, col_send, col_recv)
    halo_start(halo1)
    end_stages(2, 0)
    for load in loads[9:12]:
        load.wait()
    groups = enth.shape[1] // width
    for g in range(groups):
        values[pl.ds(g * layers, layers), :] = enth[:, g * width : (g + 1) * width]

    def rate_of(k):
        return jnp.where(k < trans[...], cold_rate, temperate_rate).astype(jnp.float32)

    def layer(k):
        return pl.ds(k, groups, stride=layers)

    def eliminate(k, carry):
        ratio, value, rate, inner_up = carry
        rate_next = rate_of(k + 1)
        inner = 0.5 * (rate + rate_next)
        pivot = inverse(1.0 + inner_up + inner + inner_up * ratio)
        value = (values[layer(k), :] + inner_up * value) * pivot
        ratio = -inner * pivot
        values[layer(k), :] = value
        ratios[layer(k), :] = ratio
        return ratio, value, rate_next, inner

    last = layers - 1

    halo_wait(halo_top2)
    for q in range(2):
        spread_edge(q, col_top_in2, edge_top)
    spread((first_top.at[0], first_top.at[1]), row_top_in2, edge_top, 0)
    new_top_temp, new_top_salt, melt_two, base_two = surface()
    mean_melt = 0.5 * (melt_one + melt_two)
    mean_base = 0.5 * (base_one + base_two)
    for load in loads[12:]:
        load.wait()

    batch = 64

    def pairs(i, carry):
        at = pl.ds(pl.multiple_of(i * batch, batch), batch)
        place = pcol[at, :]
        place_row = quotient(place, ci)
        place_col = remainder(place, ci)
        weight = pw[at, :]
        for slot, table in ((0, mean_melt), (1, mean_base)):
            found = jnp.zeros((batch, width), jnp.float32)
            for r in range(cj):
                line = jnp.broadcast_to(table[r : r + 1], (batch, ci))
                there = jnp.take_along_axis(
                    line, place_col, axis=1, mode="promise_in_bounds"
                )
                found = jnp.where(place_row == r, there, found)
            high, low = split_two(weight * found)
            pay[slot, at, pl.ds(0, width)] = high
            pay[slot, at, pl.ds(width, width)] = low
        return carry

    lax.fori_loop(0, blocks // batch, pairs, 0)
    for part in range(PARTS):
        for slot in range(2):
            sum_blocks(slot, part)

    halo2 = halo(1, row_send2, row_recv2, col_send2, col_recv2)

    def first_couple():
        halo_wait(halo1)
        for q in range(3):
            spread_edge(q, col_recv, edge)
        loop(0, chunks, functools.partial(couple, row_recv, edge))

    def first_spread():
        loop(0, chunks, functools.partial(spread, (temp, salt), row_recv, edge))

    def first_mix():
        loop(0, chunks, lambda c: mix(c, (first.at[0], first.at[1])))
        first[0, pl.ds(0, cj), :] = top_temp
        first[1, pl.ds(0, cj), :] = top_salt
        for q in range(2):
            pack(q, first.at[q], 0, row_send2, col_send2)
        halo_start(halo2)

    def second_spread():
        halo_wait(halo2)
        for q in range(2):
            spread_edge(q, col_recv2, edge)
        sources = (first.at[0], first.at[1])
        loop(0, chunks, functools.partial(spread, sources, row_recv2, edge))

    def second_mix():
        loop(0, chunks, lambda c: mix(c, (out_temp, out_salt)))
        out_temp[pl.ds(0, cj), :] = new_top_temp
        out_salt[pl.ds(0, cj), :] = new_top_salt
        saves[0].start()
        saves[1].start()

    middle = 1 + (last - 1) // 4 * 2

    def forward_first():
        rate_top = rate_of(0)
        rate_next = rate_of(1)
        inner = 0.5 * (rate_top + rate_next)
        pivot = 1.0 / (1.0 + rate_top + inner)
        value = (values[layer(0), :] + rate_top * surf[...]) * pivot
        ratio = -inner * pivot
        values[layer(0), :] = value
        ratios[layer(0), :] = ratio
        return lax.fori_loop(1, middle, eliminate, (ratio, value, rate_next, inner), unroll=2)

    def forward_rest(state):
        return lax.fori_loop(middle, last, eliminate, state, unroll=2)

    def back_terms(state):
        ratio_end, value_end, _, _ = state
        ratios[layer(last - 1), :] = -ratio_end

        def body(n, carry):
            level, slope = carry
            k = last - 2 - n
            ratio = ratios[layer(k), :]
            level = values[layer(k), :] - ratio * level
            slope = -ratio * slope
            values[layer(k), :] = level
            ratios[layer(k), :] = slope
            return level, slope

        lax.fori_loop(0, last - 1, body, (value_end, -ratio_end), unroll=2)
        last_side = values[layer(last), :]
        values[layer(last), :] = jnp.zeros((groups, width), jnp.float32)
        ratios[layer(last), :] = jnp.ones((groups, width), jnp.float32)
        return last_side

    stages = len(orders[0])

    def advance(stage, between=None):
        made = None
        for part in range(PARTS):
            for slot in range(2):
                end_stage(chains[part * 3 + slot], stage)
            if part == 0 and between is not None:
                made = between()
        if stage + 1 < stages:
            end_stages(2, stage + 1)
        return made

    first_couple()
    advance(0)
    first_spread()
    first_mix()
    state = advance(1, forward_first) if stages > 1 else forward_first()
    state = forward_rest(state)
    if stages > 2:
        advance(2)
    last_side = back_terms(state)
    second_spread()
    second_mix()
    for chain in chains:
        drain(chain, range(min(2, stages)))
    for stage in range(3, stages):
        advance(stage)
    ratio_end, value_end, _, inner_end = state

    share = 1.0 / area[...]
    sums = [
        jnp.concatenate([chains[part * 3 + slot][1][-1][...] for part in range(PARTS)], axis=0)
        for slot in range(3)
    ]
    melt_sum = sums[0] * share
    base_sum = sums[1] * share
    cover_sum = sums[2] * share
    out_melt[...] = melt_sum
    pivot = 1.0 / (1.0 + inner_end + cover_sum + inner_end * ratio_end)
    last_layer[...] = (last_side + base_sum + inner_end * value_end) * pivot
    for g in range(groups):
        rows = pl.ds(g * layers, layers)
        solved = values[rows, :] + ratios[rows, :] * last_layer[pl.ds(g, 1), :]
        out_enth[:, g * width : (g + 1) * width] = solved
    saves[2].start()
    saves[3].start()

    halo_done(halo_top1)
    halo_done(halo_top2)
    halo_done(halo1)
    halo_done(halo2)
    for chain in chains:
        drain(chain, range(min(2, stages), stages))
    for save in saves:
        save.wait()


def store(*refs):
    count = len(refs) // 3
    sems = refs[3 * count]
    inward = []
    outward = []
    for i in range(count):
        src, dst, held = refs[i], refs[count + i], refs[2 * count + i]
        inward.append(pltpu.make_async_copy(src, held, sems.at[0, i]))
        outward.append(pltpu.make_async_copy(held, dst, sems.at[1, i]))
    for copy in inward:
        copy.start()
    for first, then in zip(inward, outward):
        first.wait()
        then.start()
    for copy in outward:
        copy.wait()


def local(
    nx,
    ny,
    ocean_temp,
    ocean_salt,
    wet_mask,
    vertical_mix,
    friction,
    pressure,
    pair_column,
    pair_weight,
    block_owner,
    block_target,
    enthalpy,
    surface_enthalpy,
    transition_layer,
    column_area,
):
    levels, cj, ci = wet_mask.shape
    cells = levels * cj
    blocks, width = pair_column.shape
    layers, columns = enthalpy.shape
    targets = columns // width
    orders = stage_orders(nx, ny)
    f32 = jnp.float32
    total = nx * ny * targets
    given = (
        ocean_temp.reshape(cells, ci),
        ocean_salt.reshape(cells, ci),
        wet_mask.reshape(cells, ci),
        vertical_mix,
        friction,
        pressure,
        block_owner.reshape(1, blocks),
        block_target.reshape(1, blocks),
        pair_weight,
        transition_layer.reshape(targets, width),
        surface_enthalpy.reshape(targets, width),
        enthalpy,
        pair_column,
        column_area.reshape(targets, width),
    )
    results = (
        jax.ShapeDtypeStruct((cells, ci), f32),
        jax.ShapeDtypeStruct((cells, ci), f32),
        jax.ShapeDtypeStruct((layers, columns), f32),
        jax.ShapeDtypeStruct((targets, width), f32),
    )
    top_cells = 2 * CHUNK * cj
    scratch = [pltpu.VMEM(leaf.shape, leaf.dtype) for leaf in given]
    scratch += [pltpu.VMEM(leaf.shape, leaf.dtype) for leaf in results]
    scratch += [pltpu.SemaphoreType.DMA((len(given),)), pltpu.SemaphoreType.DMA((4,))]
    scratch += [
        pltpu.VMEM((cells + 2 * cj, ci), f32),
        pltpu.VMEM((4, cells, ci), f32),
        pltpu.VMEM((2, cells + 2 * cj, ci), f32),
        pltpu.VMEM((3, cells, ci), f32),
        pltpu.VMEM((2, cells, ci), f32),
        pltpu.VMEM((3, top_cells, ci), f32),
        pltpu.VMEM((2, top_cells, ci), f32),
        pltpu.VMEM((targets, width), f32),
        pltpu.VMEM((2, 3, levels, ci), f32),
        pltpu.VMEM((2, 3, levels, ci), f32),
        pltpu.VMEM((2, 8, cells), f32),
        pltpu.VMEM((2, 8, cells), f32),
        pltpu.VMEM((2, 2, levels, ci), f32),
        pltpu.VMEM((2, 2, levels, ci), f32),
        pltpu.VMEM((2, 8, cells), f32),
        pltpu.VMEM((2, 8, cells), f32),
        pltpu.VMEM((2, 3, CHUNK, ci), f32),
        pltpu.VMEM((2, 3, CHUNK, ci), f32),
        pltpu.VMEM((2, 8, top_cells), f32),
        pltpu.VMEM((2, 8, top_cells), f32),
        pltpu.VMEM((2, 2, CHUNK, ci), f32),
        pltpu.VMEM((2, 2, CHUNK, ci), f32),
        pltpu.VMEM((2, 8, top_cells), f32),
        pltpu.VMEM((2, 8, top_cells), f32),
        pltpu.VMEM((total, blocks), jnp.bfloat16),
        pltpu.VMEM((3, blocks, 2 * width), jnp.bfloat16),
        pltpu.VMEM((layers * targets, width), f32),
        pltpu.VMEM((layers * targets, width), f32),
    ]
    for order in (orders[0], orders[1], orders[0]) * PARTS:
        rows = live_rows(order, total // PARTS)
        scratch += [pltpu.VMEM((n, width), f32) for n in rows]
        scratch += [
            pltpu.VMEM((radix - 1, n, width), f32)
            for (_, _, radix), n in zip(order, rows[1:])
        ]
        most = max(radix for _, _, radix in order) - 1
        scratch += [pltpu.SemaphoreType.DMA((len(order), most))] * 2
    scratch += [pltpu.SemaphoreType.DMA((4, 4))] * 2
    sizes = (nx, ny, levels, cj, ci, targets, layers)
    hbm = pl.BlockSpec(memory_space=pltpu.HBM)
    made = pl.pallas_call(
        functools.partial(kernel, sizes, orders),
        out_shape=results,
        in_specs=[hbm] * len(given),
        out_specs=(hbm,) * 4,
        scratch_shapes=scratch,
        compiler_params=pltpu.CompilerParams(
            collective_id=0, has_side_effects=True, vmem_limit_bytes=LIMIT
        ),
    )(*given)
    new_temp, new_salt, new_enthalpy, ice_melt = pl.pallas_call(
        store,
        out_shape=results,
        in_specs=[hbm] * 4,
        out_specs=(hbm,) * 4,
        scratch_shapes=[pltpu.VMEM(leaf.shape, leaf.dtype) for leaf in results]
        + [pltpu.SemaphoreType.DMA((2, 4))],
        compiler_params=pltpu.CompilerParams(vmem_limit_bytes=LIMIT),
    )(*made)
    return (
        new_temp.reshape(levels, cj, ci),
        new_salt.reshape(levels, cj, ci),
        new_enthalpy,
        ice_melt.reshape(columns),
    )


def solution(mesh):
    return jax.shard_map(
        functools.partial(local, mesh.shape["gx"], mesh.shape["gy"]),
        mesh=mesh,
        in_specs=(
            P(None, "gy", "gx"),
            P(None, "gy", "gx"),
            P(None, "gy", "gx"),
            P("gy", "gx"),
            P("gy", "gx"),
            P("gy", "gx"),
            P(("gx", "gy"), None),
            P(("gx", "gy"), None),
            P(("gx", "gy"), None),
            P(("gx", "gy")),
            P(None, ("gx", "gy")),
            P(("gx", "gy")),
            P(("gx", "gy")),
            P(("gx", "gy")),
        ),
        out_specs=(
            P(None, "gy", "gx"),
            P(None, "gy", "gx"),
            P(None, ("gx", "gy")),
            P(("gx", "gy")),
        ),
        check_vma=False,
    )
```

```python
import functools

import jax
import jax.numpy as jnp
from jax import lax
from jax.experimental import pallas as pl
from jax.experimental.pallas import tpu as pltpu
from jax.sharding import PartitionSpec as P

mixing_rate = 0.2
liquidus_slope = -0.0573
liquidus_base = 0.0832
liquidus_depth = -0.000753
latent_ratio = 4.0
salt_ratio = 35.0
relax_rate = 0.1
cold_rate = 2.0
temperate_rate = 0.2

MESH = pl.DeviceIdType.MESH
CHUNK = 8
PARTS = 2
LIMIT = 62 * 1024 * 1024


def shelf_melt(surface_temp, surface_salt, friction, pressure, wet_top):
    heat_gain = jnp.where(wet_top > 0, friction, 1.0)
    salt_safe = jnp.where(wet_top > 0, surface_salt, 34.0)
    salt_gain = heat_gain / salt_ratio
    curvature = heat_gain * liquidus_slope
    linear = (
        heat_gain * (surface_temp - liquidus_base - liquidus_depth * pressure)
        + latent_ratio * salt_gain
    )
    constant = latent_ratio * salt_gain * salt_safe
    boundary_salt = (
        2.0 * constant / (linear + jnp.sqrt(linear * linear - 4.0 * curvature * constant))
    )
    boundary_temp = liquidus_slope * boundary_salt + liquidus_base + liquidus_depth * pressure
    heat_flux = heat_gain * (surface_temp - boundary_temp) * wet_top
    salt_flux = salt_gain * (salt_safe - boundary_salt) * wet_top
    return (heat_flux, salt_flux, boundary_temp * wet_top)


def quotient(value, size):
    if size & (size - 1):
        return value // size
    return lax.shift_right_logical(value, size.bit_length() - 1)


def remainder(value, size):
    return value - quotient(value, size) * size if size & (size - 1) else value & (size - 1)


def digits(axis, size):
    found = []
    base = 1
    while size > 1:
        radix = next(p for p in range(2, size + 1) if size % p == 0)
        if axis == "gx" and size == 4:
            radix = size
        found.append((axis, base, radix))
        base *= radix
        size //= radix
    return found


def stage_orders(nx, ny):
    gy = digits("gy", ny)
    gx = digits("gx", nx)
    first = gy + gx
    second = gy[:1] + gx[:1] + gy[1:] + gx[1:]
    third = gy[:1] + gx[-1:] + gy[1:] + gx[:-1]
    return (first, second, third)


def slot_of(owner, order, ny):
    coord = {"gx": quotient(owner, ny), "gy": remainder(owner, ny)}
    place = jnp.zeros_like(owner)
    for axis, base, radix in order:
        place = place * radix + remainder(quotient(coord[axis], base), radix)
    return place


def live_rows(order, total):
    rows = [total]
    for _, _, radix in order:
        rows.append(rows[-1] // radix)
    return rows


def inverse(value):
    guess = pl.reciprocal(value, approx=True)
    guess = guess * (2.0 - value * guess)
    return guess * (2.0 - value * guess)


def split_two(value):
    high = value.astype(jnp.bfloat16)
    low = (value - high.astype(jnp.float32)).astype(jnp.bfloat16)
    return high, low


def kernel(sizes, orders, *refs):
    nx, ny, levels, cj, ci, targets, layers = sizes
    refs = list(refs)

    def take(count):
        out = refs[:count]
        del refs[:count]
        return out

    given = take(14)
    results = take(4)
    held = take(14)
    (out_temp, out_salt, out_enth, out_melt) = made = take(4)
    (load_sem, save_sem) = take(2)
    saves = [
        pltpu.make_async_copy(src, dst, save_sem.at[i])
        for i, (src, dst) in enumerate(zip(made, results))
    ]
    loads = [
        pltpu.make_async_copy(src, dst, load_sem.at[i])
        for i, (src, dst) in enumerate(zip(given, held))
    ]
    for load in loads:
        load.start()
    (temp, salt, wet, vmix, fric, pres, owner, target, pw, trans, surf, enth, pcol, area) = held
    (wetp, coef, mid, edge, first) = take(5)
    (edge_top, first_top, last_layer) = take(3)
    (row_send, row_recv, col_send, col_recv) = take(4)
    (row_send2, row_recv2, col_send2, col_recv2) = take(4)
    (row_top, row_top_in, col_top, col_top_in) = take(4)
    (row_top2, row_top_in2, col_top2, col_top_in2) = take(4)
    (hot, pay, ratios, values) = take(4)
    chains = []
    for order in orders * PARTS:
        live = take(len(order) + 1)
        got = take(len(order))
        send_sem, recv_sem = take(2)
        chains.append((order, live, got, send_sem, recv_sem))
    (halo_send, halo_recv) = take(2)

    gx = lax.axis_index("gx")
    gy = lax.axis_index("gy")
    coord = {"gx": gx, "gy": gy}
    span = cj * CHUNK
    chunks = levels // CHUNK
    cells = levels * cj
    blocks = pcol.shape[0]
    width = pcol.shape[1]

    sides = (
        (gy > 0, {"gy": gy - 1}),
        (gy < ny - 1, {"gy": gy + 1}),
        (gx > 0, {"gx": gx - 1}),
        (gx < nx - 1, {"gx": gx + 1}),
    )

    for buf in (row_recv, row_recv2, row_top_in, row_top_in2):
        for side in range(2):
            @pl.when(jnp.logical_not(sides[side][0]))
            def _():
                buf[side] = jnp.zeros(buf.shape[1:], jnp.float32)
    for buf in (col_recv, col_recv2, col_top_in, col_top_in2):
        for side in range(2):
            @pl.when(jnp.logical_not(sides[2 + side][0]))
            def _():
                buf[side] = jnp.zeros(buf.shape[1:], jnp.float32)

    barrier = pltpu.get_barrier_semaphore()
    partners = 0
    for there, device in sides:
        @pl.when(there)
        def _():
            pl.semaphore_signal(barrier, inc=1, device_id=device, device_id_type=MESH)
        partners = partners + there.astype(jnp.int32)
    for axis, base, radix in orders[0]:
        mine = (coord[axis] // base) % radix
        for j in range(1, radix):
            peer = {axis: coord[axis] + ((mine + j) % radix - mine) * base}
            pl.semaphore_signal(barrier, inc=1, device_id=peer, device_id_type=MESH)
            partners = partners + 1

    zeros_pad = jnp.zeros((cj, ci), jnp.float32)
    wetp[pl.ds(0, cj), :] = zeros_pad
    wetp[pl.ds(cj + cells, cj), :] = zeros_pad
    for q in range(2):
        mid[q, pl.ds(0, cj), :] = zeros_pad
        mid[q, pl.ds(cj + cells, cj), :] = zeros_pad

    def pack(q, source, offset, rows, cols):
        count = rows.shape[2]
        rows[0, q] = source[pl.ds(offset, count, stride=cj), :]
        rows[1, q] = source[pl.ds(offset + cj - 1, count, stride=cj), :]
        turned = source[pl.ds(offset, cols.shape[2]), :].T
        cols[0, pl.ds(q, 1), :] = turned[0:1]
        cols[1, pl.ds(q, 1), :] = turned[ci - 1 : ci]

    for cols in (col_send, col_send2, col_top, col_top2):
        cols[...] = jnp.zeros(cols.shape, jnp.float32)
    first_top[...] = jnp.zeros(first_top.shape, jnp.float32)
    for load in loads[:3]:
        load.wait()
    wetp[pl.ds(cj, cells), :] = wet[...].astype(jnp.float32)

    def pack_all(rows, cols):
        pack(0, temp, 0, rows, cols)
        pack(1, salt, 0, rows, cols)
        pack(2, wetp, cj, rows, cols)

    pack_all(row_top, col_top)
    pl.semaphore_wait(barrier, partners)

    def halo(step, rows, rows_in, cols, cols_in):
        copies = []
        for side, (there, device) in enumerate(sides):
            src, dst = (rows, rows_in) if side < 2 else (cols, cols_in)
            copies.append(
                pltpu.make_async_remote_copy(
                    src_ref=src.at[side % 2],
                    dst_ref=dst.at[1 - side % 2],
                    send_sem=halo_send.at[step, side],
                    recv_sem=halo_recv.at[step, side - side % 2 + 1 - side % 2],
                    device_id=device,
                    device_id_type=MESH,
                )
            )
        return copies

    def halo_start(copies):
        for (there, _), copy in zip(sides, copies):
            @pl.when(there)
            def _():
                copy.start()

    def halo_wait(copies):
        for side, (there, _) in enumerate(sides):
            opposite = copies[side - side % 2 + 1 - side % 2]

            @pl.when(there)
            def _():
                opposite.wait_recv()

    def halo_done(copies):
        for (there, _), copy in zip(sides, copies):
            @pl.when(there)
            def _():
                copy.wait_send()

    halo_top1 = halo(2, row_top, row_top_in, col_top, col_top_in)
    halo_start(halo_top1)

    def make_copies(chain, stage):
        order, live, got, send_sem, recv_sem = chain
        axis, base, radix = order[stage]
        rows = live[stage + 1].shape[0]
        mine = (coord[axis] // base) % radix
        copies = []
        for j in range(1, radix):
            digit = (mine + j) % radix
            copies.append(
                pltpu.make_async_remote_copy(
                    src_ref=live[stage].at[pl.ds(digit * rows, rows)],
                    dst_ref=got[stage].at[j - 1],
                    send_sem=send_sem.at[stage, j - 1],
                    recv_sem=recv_sem.at[stage, j - 1],
                    device_id={axis: coord[axis] + (digit - mine) * base},
                    device_id_type=MESH,
                )
            )
        return copies

    def start_stage(chain, stage):
        for copy in make_copies(chain, stage):
            copy.start()

    def end_stage(chain, stage):
        order, live, got, _, _ = chain
        axis, base, radix = order[stage]
        rows = live[stage + 1].shape[0]
        mine = (coord[axis] // base) % radix
        total = live[stage][pl.ds(pl.multiple_of(mine * rows, rows), rows), :]
        for copy in make_copies(chain, stage):
            copy.wait_recv()
        for j in range(1, radix):
            total = total + got[stage][j - 1]
        live[stage + 1][...] = total
        if stage + 1 < len(order):
            start_stage(chain, stage + 1)

    def drain(chain, stages_done):
        for stage in stages_done:
            for copy in make_copies(chain, stage):
                copy.wait_send()

    part_rows = chains[0][1][0].shape[0]
    seg_total = part_rows * PARTS
    share_rows = targets // PARTS
    hot_rows = min(256, part_rows)

    def build_hot():
        place = target[...]
        seg = slot_of(owner[...], orders[0], ny) * share_rows + remainder(place, share_rows)
        seg = quotient(place, share_rows) * part_rows + seg

        def body(i, carry):
            start = pl.multiple_of(i * hot_rows, hot_rows)
            row = lax.broadcasted_iota(jnp.int32, (hot_rows, blocks), 0) + start
            hit = (row == seg).astype(jnp.float32)
            hot[pl.ds(start, hot_rows), :] = hit.astype(jnp.bfloat16)
            return carry

        lax.fori_loop(0, seg_total // hot_rows, body, 0)

    def placed(order):
        common = 0
        while common < len(order) and order[-1 - common] == orders[0][-1 - common]:
            common += 1
        run = share_rows
        for _, _, radix in order[len(order) - common :]:
            run *= radix
        head = orders[0][: len(order) - common]
        goals = []
        for n in range(part_rows // run):
            left = n
            at = {}
            for digit in reversed(head):
                at[digit] = left % digit[2]
                left //= digit[2]
            goal = 0
            for digit in order[: len(order) - common]:
                goal = goal * digit[2] + at[digit]
            goals.append(goal * run)
        return run, goals

    def sum_blocks(slot, part):
        order, live = chains[part * 3 + slot][:2]
        run, goals = placed(order)
        step = min(run, hot_rows)
        for start in range(0, part_rows, hot_rows):
            both = jnp.dot(
                hot[pl.ds(part * part_rows + start, hot_rows), :],
                pay[slot],
                preferred_element_type=jnp.float32,
            )
            both = both[:, :width] + both[:, width:]
            for piece in range(0, hot_rows, step):
                n, inside = divmod(start + piece, run)
                live[0][pl.ds(goals[n] + inside, step), :] = both[piece : piece + step]
        start_stage(chains[part * 3 + slot], 0)

    def end_stages(slot, stage):
        for part in range(PARTS):
            end_stage(chains[part * 3 + slot], stage)

    for load in loads[6:9]:
        load.wait()
    build_hot()
    high, low = split_two(pw[...])
    pay[2, :, pl.ds(0, width)] = high
    pay[2, :, pl.ds(width, width)] = low
    for part in range(PARTS):
        sum_blocks(2, part)
    for load in loads[3:6]:
        load.wait()

    lane = lax.broadcasted_iota(jnp.int32, (CHUNK, cj, ci), 2)
    row = lax.broadcasted_iota(jnp.int32, (CHUNK, cj, ci), 1)

    def spread_edge(q, cols_in, edge):
        turned = lax.broadcasted_iota(jnp.int32, (ci, cols_in.shape[2]), 0)
        both = jnp.where(turned == 0, cols_in[0, pl.ds(q, 1), :], cols_in[1, pl.ds(q, 1), :])
        edge[q] = both.T

    def around(x, q, c, rows_in, edge):
        start = pl.multiple_of(c * span, span)
        level = pl.ds(pl.multiple_of(c * CHUNK, CHUNK), CHUNK)
        side = edge[q, pl.ds(start, span), :].reshape(CHUNK, cj, ci)
        west = jnp.where(lane == 0, side, pltpu.roll(x, 1, 2))
        east = jnp.where(lane == ci - 1, side, pltpu.roll(x, ci - 1, 2))
        north = jnp.where(row == 0, rows_in[0, q, level, :][:, None, :], pltpu.roll(x, 1, 1))
        south = jnp.where(
            row == cj - 1, rows_in[1, q, level, :][:, None, :], pltpu.roll(x, cj - 1, 1)
        )
        return west, east, north, south

    def couple(rows_in, edge, c):
        start = pl.multiple_of(c * span, span)
        x = wetp[pl.ds(pl.multiple_of(cj + start, cj), span), :].reshape(CHUNK, cj, ci)
        for n, beside in enumerate(around(x, 2, c, rows_in, edge)):
            coef[n, pl.ds(start, span), :] = (mixing_rate * (x * beside)).reshape(span, ci)

    def spread(sources, rows_in, edge, c):
        start = pl.multiple_of(c * span, span)
        weights = [coef[n, pl.ds(start, span), :].reshape(CHUNK, cj, ci) for n in range(4)]
        for q in range(2):
            x = sources[q][pl.ds(start, span), :].reshape(CHUNK, cj, ci)
            total = x
            for weight, beside in zip(weights, around(x, q, c, rows_in, edge)):
                total = total + weight * (beside - x)
            mid[q, pl.ds(pl.multiple_of(cj + start, cj), span), :] = total.reshape(span, ci)

    def mix(c, targets_of):
        start = pl.multiple_of(c * span, span)
        up = pl.ds(start, span)
        here = pl.ds(pl.multiple_of(start + cj, cj), span)
        down = pl.ds(pl.multiple_of(start + 2 * cj, cj), span)
        rate = jnp.broadcast_to(vmix[...][None], (CHUNK, cj, ci)).reshape(span, ci)
        wet_here = rate * wetp[here, :]
        link_up = wet_here * wetp[up, :]
        link_down = wet_here * wetp[down, :]
        for q in range(2):
            x = mid[q, here, :]
            targets_of[q][pl.ds(start, span), :] = (
                x + link_down * (mid[q, down, :] - x) - link_up * (x - mid[q, up, :])
            )

    wet_top = wetp[pl.ds(cj, cj), :]

    def surface():
        link = vmix[...] * wet_top * wetp[pl.ds(2 * cj, cj), :]
        top = []
        for q in range(2):
            x = mid[q, pl.ds(cj, cj), :]
            top.append(x + link * (mid[q, pl.ds(2 * cj, cj), :] - x))
        heat, saltf, base_temp = shelf_melt(top[0], top[1], fric[...], pres[...], wet_top)
        return (
            top[0] - relax_rate * heat,
            top[1] - relax_rate * saltf,
            heat / latent_ratio,
            base_temp,
        )

    def loop(low_c, high_c, body):
        def wrapped(c, carry):
            body(c)
            return carry

        lax.fori_loop(low_c, high_c, wrapped, 0)

    halo_wait(halo_top1)
    for q in range(3):
        spread_edge(q, col_top_in, edge_top)
    couple(row_top_in, edge_top, 0)
    spread((temp, salt), row_top_in, edge_top, 0)
    mix(0, (first_top.at[0], first_top.at[1]))
    top_temp, top_salt, melt_one, base_one = surface()
    first_top[0, pl.ds(0, cj), :] = top_temp
    first_top[1, pl.ds(0, cj), :] = top_salt
    for q in range(2):
        pack(q, first_top.at[q], 0, row_top2, col_top2)
    halo_top2 = halo(3, row_top2, row_top_in2, col_top2, col_top_in2)
    halo_start(halo_top2)

    pack_all(row_send, col_send)
    halo1 = halo(0, row_send, row_recv, col_send, col_recv)
    halo_start(halo1)
    end_stages(2, 0)
    for load in loads[9:12]:
        load.wait()
    groups = enth.shape[1] // width
    for g in range(groups):
        values[pl.ds(g * layers, layers), :] = enth[:, g * width : (g + 1) * width]

    def rate_of(k):
        return jnp.where(k < trans[...], cold_rate, temperate_rate).astype(jnp.float32)

    def layer(k):
        return pl.ds(k, groups, stride=layers)

    def eliminate(k, carry):
        ratio, value, rate, inner_up = carry
        rate_next = rate_of(k + 1)
        inner = 0.5 * (rate + rate_next)
        pivot = inverse(1.0 + inner_up + inner + inner_up * ratio)
        value = (values[layer(k), :] + inner_up * value) * pivot
        ratio = -inner * pivot
        values[layer(k), :] = value
        ratios[layer(k), :] = ratio
        return ratio, value, rate_next, inner

    last = layers - 1

    halo_wait(halo_top2)
    for q in range(2):
        spread_edge(q, col_top_in2, edge_top)
    spread((first_top.at[0], first_top.at[1]), row_top_in2, edge_top, 0)
    new_top_temp, new_top_salt, melt_two, base_two = surface()
    mean_melt = 0.5 * (melt_one + melt_two)
    mean_base = 0.5 * (base_one + base_two)
    for load in loads[12:]:
        load.wait()

    batch = 64

    def pairs(i, carry):
        at = pl.ds(pl.multiple_of(i * batch, batch), batch)
        place = pcol[at, :]
        place_row = quotient(place, ci)
        place_col = remainder(place, ci)
        weight = pw[at, :]
        for slot, table in ((0, mean_melt), (1, mean_base)):
            found = jnp.zeros((batch, width), jnp.float32)
            for r in range(cj):
                line = jnp.broadcast_to(table[r : r + 1], (batch, ci))
                there = jnp.take_along_axis(
                    line, place_col, axis=1, mode="promise_in_bounds"
                )
                found = jnp.where(place_row == r, there, found)
            high, low = split_two(weight * found)
            pay[slot, at, pl.ds(0, width)] = high
            pay[slot, at, pl.ds(width, width)] = low
        return carry

    lax.fori_loop(0, blocks // batch, pairs, 0)
    for part in range(PARTS):
        for slot in range(2):
            sum_blocks(slot, part)

    halo2 = halo(1, row_send2, row_recv2, col_send2, col_recv2)

    def first_couple():
        halo_wait(halo1)
        for q in range(3):
            spread_edge(q, col_recv, edge)
        loop(0, chunks, functools.partial(couple, row_recv, edge))

    def first_spread():
        loop(0, chunks, functools.partial(spread, (temp, salt), row_recv, edge))

    def first_mix():
        loop(0, chunks, lambda c: mix(c, (first.at[0], first.at[1])))
        first[0, pl.ds(0, cj), :] = top_temp
        first[1, pl.ds(0, cj), :] = top_salt
        for q in range(2):
            pack(q, first.at[q], 0, row_send2, col_send2)
        halo_start(halo2)

    def second_spread():
        halo_wait(halo2)
        for q in range(2):
            spread_edge(q, col_recv2, edge)
        sources = (first.at[0], first.at[1])
        loop(0, chunks, functools.partial(spread, sources, row_recv2, edge))

    def second_mix():
        loop(0, chunks, lambda c: mix(c, (out_temp, out_salt)))
        out_temp[pl.ds(0, cj), :] = new_top_temp
        out_salt[pl.ds(0, cj), :] = new_top_salt
        saves[0].start()
        saves[1].start()

    middle = 1 + (last - 1) // 4 * 2

    def forward_first():
        rate_top = rate_of(0)
        rate_next = rate_of(1)
        inner = 0.5 * (rate_top + rate_next)
        pivot = 1.0 / (1.0 + rate_top + inner)
        value = (values[layer(0), :] + rate_top * surf[...]) * pivot
        ratio = -inner * pivot
        values[layer(0), :] = value
        ratios[layer(0), :] = ratio
        return lax.fori_loop(1, middle, eliminate, (ratio, value, rate_next, inner), unroll=2)

    def forward_rest(state):
        return lax.fori_loop(middle, last, eliminate, state, unroll=2)

    def back_terms(state):
        ratio_end, value_end, _, _ = state
        ratios[layer(last - 1), :] = -ratio_end

        def body(n, carry):
            level, slope = carry
            k = last - 2 - n
            ratio = ratios[layer(k), :]
            level = values[layer(k), :] - ratio * level
            slope = -ratio * slope
            values[layer(k), :] = level
            ratios[layer(k), :] = slope
            return level, slope

        lax.fori_loop(0, last - 1, body, (value_end, -ratio_end), unroll=2)
        last_side = values[layer(last), :]
        values[layer(last), :] = jnp.zeros((groups, width), jnp.float32)
        ratios[layer(last), :] = jnp.ones((groups, width), jnp.float32)
        return last_side

    stages = len(orders[0])

    def advance(stage, between=None):
        made = None
        for part in range(PARTS):
            for slot in range(2):
                end_stage(chains[part * 3 + slot], stage)
            if part == 0 and between is not None:
                made = between()
        if stage > 0:
            end_stages(2, stage)
        return made

    first_couple()
    advance(0)
    first_spread()
    first_mix()
    state = advance(1, forward_first) if stages > 1 else forward_first()
    state = forward_rest(state)
    if stages > 2:
        advance(2)
    last_side = back_terms(state)
    second_spread()
    second_mix()
    for chain in chains:
        drain(chain, range(min(2, stages)))
    for stage in range(3, stages):
        advance(stage)
    ratio_end, value_end, _, inner_end = state

    share = 1.0 / area[...]
    sums = [
        jnp.concatenate([chains[part * 3 + slot][1][-1][...] for part in range(PARTS)], axis=0)
        for slot in range(3)
    ]
    melt_sum = sums[0] * share
    base_sum = sums[1] * share
    cover_sum = sums[2] * share
    out_melt[...] = melt_sum
    pivot = 1.0 / (1.0 + inner_end + cover_sum + inner_end * ratio_end)
    last_layer[...] = (last_side + base_sum + inner_end * value_end) * pivot
    for g in range(groups):
        rows = pl.ds(g * layers, layers)
        solved = values[rows, :] + ratios[rows, :] * last_layer[pl.ds(g, 1), :]
        out_enth[:, g * width : (g + 1) * width] = solved
    saves[2].start()
    saves[3].start()

    halo_done(halo_top1)
    halo_done(halo_top2)
    halo_done(halo1)
    halo_done(halo2)
    for chain in chains:
        drain(chain, range(min(2, stages), stages))
    for save in saves:
        save.wait()


def store(*refs):
    count = len(refs) // 3
    sems = refs[3 * count]
    inward = []
    outward = []
    for i in range(count):
        src, dst, held = refs[i], refs[count + i], refs[2 * count + i]
        inward.append(pltpu.make_async_copy(src, held, sems.at[0, i]))
        outward.append(pltpu.make_async_copy(held, dst, sems.at[1, i]))
    for copy in inward:
        copy.start()
    for first, then in zip(inward, outward):
        first.wait()
        then.start()
    for copy in outward:
        copy.wait()


def local(
    nx,
    ny,
    ocean_temp,
    ocean_salt,
    wet_mask,
    vertical_mix,
    friction,
    pressure,
    pair_column,
    pair_weight,
    block_owner,
    block_target,
    enthalpy,
    surface_enthalpy,
    transition_layer,
    column_area,
):
    levels, cj, ci = wet_mask.shape
    cells = levels * cj
    blocks, width = pair_column.shape
    layers, columns = enthalpy.shape
    targets = columns // width
    orders = stage_orders(nx, ny)
    f32 = jnp.float32
    total = nx * ny * targets
    given = (
        ocean_temp.reshape(cells, ci),
        ocean_salt.reshape(cells, ci),
        wet_mask.reshape(cells, ci),
        vertical_mix,
        friction,
        pressure,
        block_owner.reshape(1, blocks),
        block_target.reshape(1, blocks),
        pair_weight,
        transition_layer.reshape(targets, width),
        surface_enthalpy.reshape(targets, width),
        enthalpy,
        pair_column,
        column_area.reshape(targets, width),
    )
    results = (
        jax.ShapeDtypeStruct((cells, ci), f32),
        jax.ShapeDtypeStruct((cells, ci), f32),
        jax.ShapeDtypeStruct((layers, columns), f32),
        jax.ShapeDtypeStruct((targets, width), f32),
    )
    top_cells = 2 * CHUNK * cj
    scratch = [pltpu.VMEM(leaf.shape, leaf.dtype) for leaf in given]
    scratch += [pltpu.VMEM(leaf.shape, leaf.dtype) for leaf in results]
    scratch += [pltpu.SemaphoreType.DMA((len(given),)), pltpu.SemaphoreType.DMA((4,))]
    scratch += [
        pltpu.VMEM((cells + 2 * cj, ci), f32),
        pltpu.VMEM((4, cells, ci), f32),
        pltpu.VMEM((2, cells + 2 * cj, ci), f32),
        pltpu.VMEM((3, cells, ci), f32),
        pltpu.VMEM((2, cells, ci), f32),
        pltpu.VMEM((3, top_cells, ci), f32),
        pltpu.VMEM((2, top_cells, ci), f32),
        pltpu.VMEM((targets, width), f32),
        pltpu.VMEM((2, 3, levels, ci), f32),
        pltpu.VMEM((2, 3, levels, ci), f32),
        pltpu.VMEM((2, 8, cells), f32),
        pltpu.VMEM((2, 8, cells), f32),
        pltpu.VMEM((2, 2, levels, ci), f32),
        pltpu.VMEM((2, 2, levels, ci), f32),
        pltpu.VMEM((2, 8, cells), f32),
        pltpu.VMEM((2, 8, cells), f32),
        pltpu.VMEM((2, 3, CHUNK, ci), f32),
        pltpu.VMEM((2, 3, CHUNK, ci), f32),
        pltpu.VMEM((2, 8, top_cells), f32),
        pltpu.VMEM((2, 8, top_cells), f32),
        pltpu.VMEM((2, 2, CHUNK, ci), f32),
        pltpu.VMEM((2, 2, CHUNK, ci), f32),
        pltpu.VMEM((2, 8, top_cells), f32),
        pltpu.VMEM((2, 8, top_cells), f32),
        pltpu.VMEM((total, blocks), jnp.bfloat16),
        pltpu.VMEM((3, blocks, 2 * width), jnp.bfloat16),
        pltpu.VMEM((layers * targets, width), f32),
        pltpu.VMEM((layers * targets, width), f32),
    ]
    for order in orders * PARTS:
        rows = live_rows(order, total // PARTS)
        scratch += [pltpu.VMEM((n, width), f32) for n in rows]
        scratch += [
            pltpu.VMEM((radix - 1, n, width), f32)
            for (_, _, radix), n in zip(order, rows[1:])
        ]
        most = max(radix for _, _, radix in order) - 1
        scratch += [pltpu.SemaphoreType.DMA((len(order), most))] * 2
    scratch += [pltpu.SemaphoreType.DMA((4, 4))] * 2
    sizes = (nx, ny, levels, cj, ci, targets, layers)
    hbm = pl.BlockSpec(memory_space=pltpu.HBM)
    made = pl.pallas_call(
        functools.partial(kernel, sizes, orders),
        out_shape=results,
        in_specs=[hbm] * len(given),
        out_specs=(hbm,) * 4,
        scratch_shapes=scratch,
        compiler_params=pltpu.CompilerParams(
            collective_id=0, has_side_effects=True, vmem_limit_bytes=LIMIT
        ),
    )(*given)
    new_temp, new_salt, new_enthalpy, ice_melt = pl.pallas_call(
        store,
        out_shape=results,
        in_specs=[hbm] * 4,
        out_specs=(hbm,) * 4,
        scratch_shapes=[pltpu.VMEM(leaf.shape, leaf.dtype) for leaf in results]
        + [pltpu.SemaphoreType.DMA((2, 4))],
        compiler_params=pltpu.CompilerParams(vmem_limit_bytes=LIMIT),
    )(*made)
    return (
        new_temp.reshape(levels, cj, ci),
        new_salt.reshape(levels, cj, ci),
        new_enthalpy,
        ice_melt.reshape(columns),
    )


def solution(mesh):
    return jax.shard_map(
        functools.partial(local, mesh.shape["gx"], mesh.shape["gy"]),
        mesh=mesh,
        in_specs=(
            P(None, "gy", "gx"),
            P(None, "gy", "gx"),
            P(None, "gy", "gx"),
            P("gy", "gx"),
            P("gy", "gx"),
            P("gy", "gx"),
            P(("gx", "gy"), None),
            P(("gx", "gy"), None),
            P(("gx", "gy"), None),
            P(("gx", "gy")),
            P(None, ("gx", "gy")),
            P(("gx", "gy")),
            P(("gx", "gy")),
            P(("gx", "gy")),
        ),
        out_specs=(
            P(None, "gy", "gx"),
            P(None, "gy", "gx"),
            P(None, ("gx", "gy")),
            P(("gx", "gy")),
        ),
        check_vma=False,
    )
```
